512 devices in a mesh: gx: 32 (over x, z), gy: 16 (over y, core).
Axes of the slice: x: 4, y: 8, z: 8, core: 2. Of those that a mesh axis runs over, the one named last changes fastest.
Arguments:
- charges: float32 [1048576], P(('gx', 'gy')), may hold values from 0 to 6
- regions: int32 [1048576], P(('gx', 'gy')), may hold values from 0 to 7
- inv_permittivity: float32 [8], replicated, may hold values from 0.25 to 1
- projection: float32 [16384, 8192], P(('gx', 'gy')), may hold values from -0.21 to 0.21
- slab_owner: int32 [16384], P(('gx', 'gy')), may hold values from 0 to 31, as said below
- brick_index: int32 [16384], P(('gx', 'gy')), may hold values from 0 to 511
- near_tiles: float32 [16384, 4096], P(('gx', 'gy')), may hold values from -0.375 to 0.375
- near_target: int32 [16384], P(('gx', 'gy')), may hold values from 0 to 31
- near_source: int32 [16384], P(('gx', 'gy')), may hold values from 0 to 31
Outputs:
- potential: float32 [1048576], P(('gx', 'gy'))
The draws below stay inside these ranges and needn't reach their ends.
Inputs may be any that keep to these rules, and one draw needn't show every extreme that they name: Exactly 22 clusters of each device have slab_owner different from the device's gx index; at most 2 of them name any one slab, and on every device at least one slab is named by exactly 2 of them. `near_target`: an index among the clusters of the block's own device. `near_source`: an index among the clusters of the block's own device.
All inputs are finite; a program needn't handle non-finite values.
Results may differ from the reference program's by a relative error of at most 0.00011.
Values sent between devices are 32-bit elements; how exact they have to be, the bound alone decides.
A program may use at most 64 MiB of HBM per device.

```python
import math
import jax
import jax.numpy as jnp
from jax import lax

CP = 64
BLOCK_SPAN_ABSCIS = 4
BY = 4
BZ = 8
SX = 16
SY = 32
G3 = 256
NREG = 8
CAP = 2
NC = 32
ZC = 128
BP = 128
NB = 512
NR = 22
CLUSTERS = 16384
TILES = 16384
N_GX = 32
N_GY = 16
DEVICES = 512


def brick_numbers(key):
    return jax.random.randint(jax.random.fold_in(key, 23), (CLUSTERS,), 0, NB, dtype=jnp.int32)


def draw_brick_index(key, part):
    return brick_numbers(key)


def draw_charges(key, part):
    key = jax.random.fold_in(key, 5)
    stored_amounts = jax.random.uniform(key, (CLUSTERS * CP,), jnp.float32, -1.2, 1.2)
    return 1.5 * jnp.exp(stored_amounts)


def draw_projection(key, part):
    numbers = brick_numbers(key)
    key = jax.random.fold_in(key, 29)
    parity = numbers // (SY // BY * (ZC // BZ)) % 2
    evenness_multiplier = 1.0 - 2.0 * parity.astype(jnp.float32)
    lattice_shift = jnp.arange(BP, dtype=jnp.int32) // (BY * BZ)
    modulating_phasor = jnp.where(lattice_shift < BLOCK_SPAN_ABSCIS // 2, 1.0, -1.0).astype(jnp.float32)
    smoothing_width_length = jax.random.uniform(key, (CLUSTERS, CP, BP), jnp.float32, 0.4, 1.6)
    flipping_polarity = 0.35
    stored_amounts = 0.08 * modulating_phasor[None, None, :] * (1.0 + flipping_polarity * evenness_multiplier)[:, None, None] * smoothing_width_length
    return stored_amounts.reshape(CLUSTERS, CP * BP)


def draw_slab_owner(key, part):
    key = jax.random.fold_in(key, 11)

    def one_device(device_key, device):
        first_key, second_key, third_key = jax.random.split(device_key, 3)
        chosen = jax.random.randint(first_key, (), 1, N_GX)
        spread = jnp.arange(N_GX - 2, dtype=jnp.int32)
        others = 1 + (chosen + spread) % (N_GX - 1)
        offset_pool = jax.random.permutation(second_key, jnp.tile(others, CAP))
        offsets = jnp.concatenate([jnp.full((CAP,), chosen, jnp.int32), offset_pool[:NR - CAP]])
        placement = jax.random.permutation(third_key, NC)
        offset_map = jnp.zeros((NC,), jnp.int32).at[placement[:NR]].set(offsets)
        home_row = device // N_GY
        return (home_row + offset_map) % N_GX
    device_keys = jax.random.split(key, DEVICES)
    return jax.vmap(one_device)(device_keys, jnp.arange(DEVICES, dtype=jnp.int32)).reshape(-1)


def set_ends(drawn, own_key, least, largest):
    longest = drawn.shape.index(max(drawn.shape))
    spots = []
    for shift in (0, 1):
        where = [jax.random.randint(jax.random.fold_in(own_key, axis), (), 0, length) for axis, length in enumerate(drawn.shape)]
        where[longest] = (where[longest] + shift) % drawn.shape[longest]
        spots.append(tuple(where))
    return drawn.at[spots[0]].set(least).at[spots[1]].set(largest)


def levels(own_key, dims, pieces, low, high):
    def one(axis_at, parts):
        heights = jax.random.uniform(jax.random.fold_in(jax.random.fold_in(own_key, 6), axis_at), (parts,), jnp.float32, low / len(pieces), high / len(pieces))
        return jnp.repeat(jnp.exp(heights), dims[axis_at] // parts).reshape((-1,) + (1,) * (len(dims) - axis_at - 1))

    loudness = one(*pieces[0])
    for cut in pieces[1:]:
        loudness = loudness * one(*cut)
    return loudness


def centred(key, extent, deviation, limit, pieces=(), kind=jnp.bfloat16):
    loudness = levels(key, extent, pieces, -0.22, 0.18) if pieces else 1.0
    array = jax.random.normal(key, extent, jnp.float32) * deviation * loudness
    return jnp.minimum(jnp.maximum(array, -limit), limit).astype(kind)


def setup_inputs(seed: int = 0) -> dict:
    splits = jax.random.split(jax.random.key(seed), 10)
    charges = draw_charges(jax.random.fold_in(splits[9], 71), 0)
    regions = set_ends(jax.random.randint(splits[1], (CLUSTERS * CP,), 0, NREG), jax.random.fold_in(splits[1], 1), 0, NREG - 1).astype(jnp.int32)
    inv_permittivity = jnp.clip(jnp.exp(jax.random.uniform(splits[2], (NREG,), jnp.float32, math.log(0.25), math.log(1.0))), 0.25, 1.0)
    projection = draw_projection(jax.random.fold_in(splits[9], 71), 0)
    slab_owner = draw_slab_owner(jax.random.fold_in(splits[9], 71), 0)
    brick_index = draw_brick_index(jax.random.fold_in(splits[9], 71), 0)
    near_tiles = centred(splits[6], (TILES, CP * CP), (4 * CP) ** -0.5, 0.375, ((0, 512),), jnp.float32)
    near_target = set_ends(jax.random.randint(splits[7], (TILES,), 0, NC), jax.random.fold_in(splits[7], 1), 0, NC - 1).astype(jnp.int32)
    near_source = set_ends(jax.random.randint(splits[8], (TILES,), 0, NC), jax.random.fold_in(splits[8], 1), 0, NC - 1).astype(jnp.int32)
    return {"charges": charges, "regions": regions, "inv_permittivity": inv_permittivity, "projection": projection, "slab_owner": slab_owner, "brick_index": brick_index, "near_tiles": near_tiles, "near_target": near_target, "near_source": near_source}


screening = 0.001
highest = lax.Precision.HIGHEST


def screened_kernel(freq_x, freq_y, freq_z, full_x, full_y, full_z):
    along_x = 4.0 * jnp.square(jnp.sin(freq_x.astype(jnp.float32) * (math.pi / full_x)))
    along_y = 4.0 * jnp.square(jnp.sin(freq_y.astype(jnp.float32) * (math.pi / full_y)))
    along_z = 4.0 * jnp.square(jnp.sin(freq_z.astype(jnp.float32) * (math.pi / full_z)))
    return 1.0 / (along_x + along_y + along_z + screening)


def reference(charges, regions, inv_permittivity, projection, slab_owner, brick_index, near_tiles, near_target, near_source):
    full_x = SX * N_GX
    full_y = SY * N_GY
    scaled = charges * inv_permittivity[regions]
    charge_rows = scaled.reshape(CLUSTERS, CP)
    blocks = projection.reshape(CLUSTERS, CP, BP)
    bricks = jnp.einsum("cpm,cp->cm", blocks, charge_rows, precision=highest)
    cluster_ids = jnp.arange(CLUSTERS, dtype=jnp.int32)
    column = (cluster_ids // NC) % N_GY
    depth_bricks = ZC // BZ
    line_bricks = SY // BY
    brick_x = brick_index // (line_bricks * depth_bricks)
    brick_y = (brick_index // depth_bricks) % line_bricks
    brick_z = brick_index % depth_bricks
    brick_point = jnp.arange(BP, dtype=jnp.int32)
    cell_x = slab_owner[:, None] * SX + brick_x[:, None] * BLOCK_SPAN_ABSCIS + (brick_point // (BY * BZ))[None, :]
    cell_y = column[:, None] * SY + brick_y[:, None] * BY + ((brick_point // BZ) % BY)[None, :]
    cell_z = brick_z[:, None] * BZ + (brick_point % BZ)[None, :]
    flat_index = ((cell_x * full_y + cell_y) * G3 + cell_z).reshape(-1)
    charge_grid = jnp.zeros((full_x * full_y * G3,), jnp.float32).at[flat_index].add(bricks.reshape(-1))
    charge_grid = charge_grid.reshape(full_x, full_y, G3)
    kernel = screened_kernel(jnp.arange(full_x, dtype=jnp.int32)[:, None, None],
                             jnp.arange(full_y, dtype=jnp.int32)[None, :, None],
                             jnp.arange(G3, dtype=jnp.int32)[None, None, :], full_x, full_y, G3)
    potential_field = jnp.real(jnp.fft.ifftn(jnp.fft.fftn(charge_grid) * kernel)).astype(jnp.float32)
    samples = potential_field.reshape(-1)[flat_index].reshape(CLUSTERS, BP)
    tile_device = jnp.arange(TILES, dtype=jnp.int32) // NC
    source_rows = charge_rows[tile_device * NC + near_source]
    target_rows = tile_device * NC + near_target
    contrib = jnp.einsum("tpq,tq->tp", near_tiles.reshape(TILES, CP, CP), source_rows, precision=highest)
    near_field = jnp.zeros((CLUSTERS, CP), jnp.float32).at[target_rows].add(contrib)
    far_field = jnp.einsum("cpm,cm->cp", blocks, samples, precision=highest)
    return (far_field + near_field).reshape(-1)
```

```python
import functools
import math

import jax
import jax.numpy as jnp
import numpy as np
from jax import lax
from jax.experimental import pallas as pl
from jax.experimental.pallas import tpu as pltpu
from jax.sharding import PartitionSpec as P

CP = 64
NREG = 8
N_GX = 32
N_GY = 16
NC = 32
BP = 128
FULL = 512
EMPTY = 512.0
SCREENING = 0.001

F32 = jnp.float32
BF16 = jnp.bfloat16
HIGHEST = lax.Precision.HIGHEST
MESH = pl.DeviceIdType.MESH

NN = (((1,), (0,)), ((), ()))
NT = (((1,), (1,)), ((), ()))


@functools.lru_cache(maxsize=None)
def host_tables():
    n = np.arange(FULL)
    angle = (n[:, None] * n[None, :] % FULL) * (2.0 * math.pi / FULL)
    natural = (np.cos(angle) + np.sin(angle)).astype(np.float32)
    dy, gy, by = np.meshgrid(np.arange(4), np.arange(N_GY), np.arange(8), indexing="ij")
    turned = natural[(gy * 32 + by * 4 + dy).reshape(-1)]

    def halves(table):
        high = table.astype(BF16)
        low = (table - high.astype(np.float32)).astype(BF16)
        return np.stack([high, low])

    along = 4.0 * np.sin(n * (math.pi / FULL)) ** 2
    a = along[:, None] + along[None, :] + SCREENING
    root = np.sqrt(a * (a + 4.0))
    decay = 2.0 / (2.0 + a + root)
    gain = 1.0 / (root * FULL * FULL)
    point = np.arange(BP)
    dx, dy, dz = point // 32, point // 8 % 4, point % 8
    lane = np.arange(4 * BP)
    spread = (
        (dx[:, None] == lane % 4)
        & (dy[:, None] == lane // 128)
        & (dz[:, None] == lane // 16 % 8)
    )
    return (
        halves(natural),
        halves(turned),
        decay.astype(np.float32),
        gain.astype(np.float32),
        spread.astype(BF16),
        np.ascontiguousarray(spread.T).astype(BF16),
    )


def halves(value):
    high = value.astype(BF16)
    return high, (value - high.astype(F32)).astype(BF16)


def product(left, right, dims):
    return (
        lax.dot_general(left[0], right[0], dims, preferred_element_type=F32)
        + lax.dot_general(left[0], right[1], dims, preferred_element_type=F32)
        + lax.dot_general(left[1], right[0], dims, preferred_element_type=F32)
    )


def picked(value, table, dims):
    high, low = halves(value)
    return lax.dot_general(high, table, dims, preferred_element_type=F32) + lax.dot_general(
        low, table, dims, preferred_element_type=F32
    )


def picked_right(table, value, dims):
    high, low = halves(value)
    return lax.dot_general(table, high, dims, preferred_element_type=F32) + lax.dot_general(
        table, low, dims, preferred_element_type=F32
    )


def lanes(shape):
    return lax.broadcasted_iota(jnp.int32, shape, 1)


def rows(shape):
    return lax.broadcasted_iota(jnp.int32, shape, 0)


def lane_sums(leaf, first, count):
    if count == 1:
        return leaf(first)
    half = count // 2
    left = lane_sums(leaf, first, half)
    right = lane_sums(leaf, first + half, half)
    upper = (lanes(left.shape) & half) != 0
    return jnp.where(upper, right, left) + pltpu.roll(
        jnp.where(upper, left, right), 128 - half, 1
    )


def swap_blocks(parts):
    parts = list(parts)
    block = lanes(parts[0].shape) // 16
    for bit in (4, 2, 1):
        upper = (block & bit) != 0
        for i in range(8):
            if i & bit:
                continue
            a, b = parts[i], parts[i | bit]
            parts[i] = jnp.where(upper, pltpu.roll(b, 16 * bit, 1), a)
            parts[i | bit] = jnp.where(upper, b, pltpu.roll(a, 128 - 16 * bit, 1))
    return parts


def start_all(count, axis, me, source, target, send_sem, recv_sem):
    def step(i, carry):
        other = lax.rem(me + i, count)
        pltpu.make_async_remote_copy(
            src_ref=source(other),
            dst_ref=target(me),
            send_sem=send_sem,
            recv_sem=recv_sem,
            device_id={axis: other},
            device_id_type=MESH,
        ).start()
        return carry

    lax.fori_loop(1, count, step, 0)


def wait_for(part, sem):
    pltpu.make_async_copy(part, part, sem).wait()


def body(
    charges_ref,
    regions_ref,
    inv_ref,
    owner_ref,
    index_ref,
    target_ref,
    source_ref,
    projection_hbm,
    tiles_hbm,
    hx_hbm,
    hy_hbm,
    decay_hbm,
    gain_hbm,
    spread_hbm,
    gather_hbm,
    out_ref,
    projection_ref,
    tiles_ref,
    hx_ref,
    hy_ref,
    decay_ref,
    gain_ref,
    spread_ref,
    gather_ref,
    rows_ref,
    send_b,
    recv_b,
    send_g,
    recv_g,
    send_x,
    recv_x,
    send_s,
    recv_s,
    send_t,
    recv_t,
    send_r,
    recv_r,
    send_f,
    recv_f,
    send_q,
    recv_q,
    local_sem,
    send_sem,
    recv_sem,
):
    gx = lax.axis_index("gx")
    gy = lax.axis_index("gy")
    barrier = pltpu.get_barrier_semaphore()

    def greet(count, axis, me):
        def step(i, carry):
            pl.semaphore_signal(
                barrier, inc=1, device_id={axis: lax.rem(me + i, count)}, device_id_type=MESH
            )
            return carry

        lax.fori_loop(1, count, step, 0)

    greet(N_GX, "gx", gx)
    greet(N_GY, "gy", gy)

    ky_rows = pl.ds(pl.multiple_of(gx * 16, 16), 16)
    loads = [
        pltpu.make_async_copy(source, target, local_sem.at[i])
        for i, (source, target) in enumerate(
            [
                (projection_hbm, projection_ref),
                (tiles_hbm, tiles_ref),
                (spread_hbm, spread_ref),
                (hy_hbm, hy_ref),
                (hx_hbm, hx_ref),
                (decay_hbm.at[ky_rows], decay_ref),
                (gain_hbm.at[ky_rows], gain_ref),
                (gather_hbm, gather_ref),
            ]
        )
    ]
    for load in loads:
        load.start()

    regions = regions_ref[...]
    factor = jnp.zeros(regions.shape, F32)
    for k in range(NREG):
        factor = jnp.where(regions == k, inv_ref[k], factor)
    scaled = charges_ref[...] * factor
    rows_ref[pl.ds(0, 16, stride=2), :] = scaled
    rows_ref[pl.ds(1, 16, stride=2), :] = pltpu.roll(scaled, 64, 1)
    charge_rows = rows_ref[...]

    own_row = owner_ref[...].astype(F32)
    index_row = index_ref[...].astype(F32)
    shape = (NC, NC)
    eye = rows(shape) == lanes(shape)
    own_col = jnp.sum(jnp.where(eye, own_row, 0.0), axis=1, keepdims=True)
    index_col = jnp.sum(jnp.where(eye, index_row, 0.0), axis=1, keepdims=True)
    here = gx.astype(F32)
    remote_col = own_col != here
    remote_row = own_row != here
    same = jnp.where((own_col == own_row) & (rows(shape) < lanes(shape)) & remote_col, 1.0, 0.0)
    rank_row = jnp.sum(same, axis=0, keepdims=True)
    slots = (4 * N_GX, NC)
    slot = rows(slots)
    chosen = jnp.where(
        (own_row == (slot // 4).astype(F32)) & (rank_row == (slot % 2).astype(F32)) & remote_row,
        1.0,
        0.0,
    )
    filled = jnp.sum(chosen, axis=1, keepdims=True)
    sent_index = jnp.sum(chosen * index_row, axis=1, keepdims=True) + (1.0 - filled) * EMPTY
    is_value = rows((4 * N_GX, BP)) % 4 < 2

    loads[0].wait()
    bricks = charge_rows[:, 0:1] * projection_ref[:, 0:BP]
    for p in range(1, CP):
        bricks = bricks + charge_rows[:, p : p + 1] * projection_ref[:, p * BP : (p + 1) * BP]
    sent = lax.dot_general(chosen, bricks, NN, precision=HIGHEST, preferred_element_type=F32)
    send_b[...] = jnp.where(is_value, sent, sent_index).reshape(N_GX, 4, BP)

    pl.semaphore_wait(barrier, N_GX - 1 + N_GY - 1)
    start_all(
        N_GX, "gx", gx, lambda d: send_b.at[d], lambda m: recv_b.at[m], send_sem.at[0], recv_sem.at[0]
    )
    recv_b[gx] = send_b[gx]

    loads[1].wait()
    from_source = jnp.where(
        jnp.sum(jnp.where(eye, source_ref[...].astype(F32), 0.0), axis=1, keepdims=True)
        == lanes(shape).astype(F32),
        1.0,
        0.0,
    )
    sources = lax.dot_general(
        from_source, charge_rows, NN, precision=HIGHEST, preferred_element_type=F32
    )
    lower = lanes((NC, BP)) < CP
    sources = jnp.where(lower, sources, pltpu.roll(sources, CP, 1))

    def near_part(p):
        part = tiles_ref[:, p // 2 * BP : (p // 2 + 1) * BP] * sources
        return jnp.where(lower if p % 2 == 0 else jnp.logical_not(lower), part, 0.0)

    contrib = lane_sums(near_part, 0, CP)
    contrib = contrib + pltpu.roll(contrib, CP, 1)
    to_target = jnp.where(rows(shape).astype(F32) == target_ref[...].astype(F32), 1.0, 0.0)
    near_field = lax.dot_general(
        to_target, contrib, NN, precision=HIGHEST, preferred_element_type=F32
    )

    loads[2].wait()
    wait_for(recv_b.at[0 : N_GX - 1], recv_sem.at[0])
    arrived = recv_b[...].reshape(4 * N_GX, BP)
    arrived_index = jnp.where(is_value, pltpu.roll(arrived, 4 * N_GX - 2, 0), EMPTY)
    arrived = jnp.where(is_value, arrived, 0.0)
    kept_index = jnp.where(remote_col, EMPTY, index_col) + jnp.zeros((NC, BP), F32)
    pad = 4 * N_GX - NC
    all_index = jnp.concatenate(
        [arrived_index, kept_index, jnp.full((pad, BP), EMPTY, F32)], axis=0
    ).astype(jnp.int32)
    values = jnp.concatenate([arrived, bricks, jnp.zeros((pad, BP), F32)], axis=0)
    lane = lanes(all_index.shape)
    in_cell = jnp.where((all_index & 15) * 8 + ((all_index >> 4) & 7) == lane, 1.0, 0.0)
    in_plane = (all_index >> 7) == ((lane >> 2) & 3)
    in_plane = jnp.concatenate([in_plane] * 4, axis=1)
    placed = jnp.where(in_plane, picked(values, spread_ref[...], NN), 0.0)
    send_g[...] = picked_right(in_cell.T.astype(BF16), placed, NN)
    start_all(
        N_GY,
        "gy",
        gy,
        lambda d: send_g.at[pl.ds(pl.multiple_of(d * 8, 8), 8), :],
        lambda m: recv_g.at[pl.ds(pl.multiple_of(m * 8, 8), 8), :],
        send_sem.at[1],
        recv_sem.at[1],
    )
    own = pl.ds(pl.multiple_of(gy * 8, 8), 8)
    recv_g[own, :] = send_g[own, :]

    loads[3].wait()
    wait_for(recv_g.at[0 : 8 * (N_GY - 1), :], recv_sem.at[1])
    turned = jnp.concatenate([recv_g[:, d * BP : (d + 1) * BP].T for d in range(4)], axis=1)
    along_y = product(halves(turned), (hy_ref[0], hy_ref[1]), NN)
    for k in range(4):
        parts = swap_blocks(
            [along_y[z * 16 : (z + 1) * 16, k * 128 : (k + 1) * 128] for z in range(8)]
        )
        for g in range(8):
            send_x[k * 8 + g] = parts[g]
    start_all(
        N_GX, "gx", gx, lambda d: send_x.at[d], lambda m: recv_x.at[m], send_sem.at[2], recv_sem.at[2]
    )
    recv_x[gx] = send_x[gx]

    loads[4].wait()
    loads[5].wait()
    loads[6].wait()
    decay = decay_ref[...]
    gain = gain_ref[...]
    powers = [None, decay]
    for k in range(2, 9):
        powers.append(powers[k // 2] * powers[k - k // 2])
    backward = gy // 8
    tile = decay_ref[
        pl.ds(pl.multiple_of(gy // 4 % 2 * 8, 8), 8), pl.ds(pl.multiple_of(gy % 4 * 128, 128), 128)
    ]
    for _ in range(3):
        tile = tile * tile
    tile_16 = tile
    for _ in range(4):
        tile_16 = tile_16 * tile_16
    around = tile_16 / (1.0 - tile_16 * tile_16)

    wait_for(recv_x.at[0 : N_GX - 1], recv_sem.at[2])
    turned = recv_x[...].reshape(FULL, BP).T
    along_x = product(halves(turned), (hx_ref[0], hx_ref[1]), NN)

    layer = [along_x[z * 16 : (z + 1) * 16, :] for z in range(8)]
    forth = [layer[0]]
    for z in range(1, 8):
        forth.append(decay * forth[-1] + layer[z])
    back = [layer[7]]
    for z in range(6, -1, -1):
        back.insert(0, decay * back[0] + layer[z])
    for d in range(N_GY):
        end = forth[7] if d < 8 else back[0]
        r, c = d // 4 % 2 * 8, d % 4 * 128
        send_s[d] = end[r : r + 8, c : c + 128]
    start_all(
        N_GY, "gy", gy, lambda d: send_s.at[d], lambda m: recv_s.at[m], send_sem.at[3], recv_sem.at[3]
    )
    recv_s[gy] = send_s[gy]
    inner = [gain * (forth[z] + back[z] - layer[z]) for z in range(8)]
    wait_for(recv_s.at[0 : N_GY - 1], recv_sem.at[3])
    order = [m + backward * (N_GY - 1 - 2 * m) for m in range(N_GY)]
    total = recv_s[order[0]]
    for m in range(1, N_GY):
        total = tile * total + recv_s[order[m]]
    carry = around * total
    for m in range(N_GY):
        send_t[order[m]] = carry
        if m < N_GY - 1:
            carry = tile * carry + recv_s[order[m]]
    start_all(
        N_GY, "gy", gy, lambda d: send_t.at[d], lambda m: recv_t.at[m], send_sem.at[4], recv_sem.at[4]
    )
    recv_t[gy] = send_t[gy]
    wait_for(recv_t.at[0 : N_GY - 1], recv_sem.at[4])

    def whole(first):
        return jnp.concatenate(
            [
                jnp.concatenate([recv_t[first + r * 4 + c] for c in range(4)], axis=1)
                for r in range(2)
            ],
            axis=0,
        )

    from_below = gain * whole(0)
    from_above = gain * whole(8)
    solved = jnp.concatenate(
        [inner[z] + from_below * powers[z + 1] + from_above * powers[8 - z] for z in range(8)],
        axis=0,
    )

    send_r[...] = product((hx_ref[0], hx_ref[1]), halves(solved), NT).reshape(N_GX, 16, BP)
    start_all(
        N_GX, "gx", gx, lambda d: send_r.at[d], lambda m: recv_r.at[m], send_sem.at[5], recv_sem.at[5]
    )
    recv_r[gx] = send_r[gx]
    wait_for(recv_r.at[0 : N_GX - 1], recv_sem.at[5])
    columns = []
    for k in range(4):
        columns.append(
            jnp.concatenate(swap_blocks([recv_r[k * 8 + g] for g in range(8)]), axis=0)
        )
    turned = halves(jnp.concatenate(columns, axis=1))

    field = product((hy_ref[0], hy_ref[1]), turned, NT)
    for d in range(4):
        send_f[:, d * BP : (d + 1) * BP] = field[d * BP : (d + 1) * BP, :]
    start_all(
        N_GY,
        "gy",
        gy,
        lambda d: send_f.at[pl.ds(pl.multiple_of(d * 8, 8), 8), :],
        lambda m: recv_f.at[pl.ds(pl.multiple_of(m * 8, 8), 8), :],
        send_sem.at[6],
        recv_sem.at[6],
    )
    recv_f[own, :] = send_f[own, :]
    loads[7].wait()
    wait_for(recv_f.at[0 : 8 * (N_GY - 1), :], recv_sem.at[6])

    lines = picked_right(in_cell.astype(BF16), recv_f[...], NN)
    samples = picked(jnp.where(in_plane, lines, 0.0), gather_ref[...], NN)
    send_q[...] = samples[0 : 4 * N_GX].reshape(N_GX, 4, BP)
    start_all(
        N_GX, "gx", gx, lambda d: send_q.at[d], lambda m: recv_q.at[m], send_sem.at[7], recv_sem.at[7]
    )
    recv_q[gx] = send_q[gx]
    taken = jnp.where(rows(slots) % 4 < 2, chosen, 0.0)
    taken = jnp.concatenate([taken, jnp.zeros((4 * N_GX, BP - NC), F32)], axis=1).T
    wait_for(recv_q.at[0 : N_GX - 1], recv_sem.at[7])
    returned = picked_right(taken.astype(BF16), recv_q[...].reshape(4 * N_GX, BP), NN)
    samples = samples[4 * N_GX : 4 * N_GX + NC] + returned[0:NC]

    def far_part(p):
        return projection_ref[:, p * BP : (p + 1) * BP] * samples

    far_field = lane_sums(far_part, 0, CP)
    far_field = far_field + pltpu.roll(far_field, CP, 1)
    rows_ref[...] = far_field + near_field
    even = rows_ref[pl.ds(0, 16, stride=2), :]
    odd = rows_ref[pl.ds(1, 16, stride=2), :]
    out_ref[...] = jnp.where(lanes((16, BP)) < CP, even, pltpu.roll(odd, CP, 1))

    wait_for(send_b.at[0 : N_GX - 1], send_sem.at[0])
    wait_for(send_g.at[0 : 8 * (N_GY - 1), :], send_sem.at[1])
    wait_for(send_x.at[0 : N_GX - 1], send_sem.at[2])
    wait_for(send_s.at[0 : N_GY - 1], send_sem.at[3])
    wait_for(send_t.at[0 : N_GY - 1], send_sem.at[4])
    wait_for(send_r.at[0 : N_GX - 1], send_sem.at[5])
    wait_for(send_f.at[0 : 8 * (N_GY - 1), :], send_sem.at[6])
    wait_for(send_q.at[0 : N_GX - 1], send_sem.at[7])


def on_device(
    charges,
    regions,
    inv_permittivity,
    projection,
    slab_owner,
    brick_index,
    near_tiles,
    near_target,
    near_source,
):
    hx, hy, decay, gain, spread, gather = (jnp.asarray(t) for t in host_tables())
    vmem = pl.BlockSpec(memory_space=pltpu.VMEM)
    anywhere = pl.BlockSpec(memory_space=pl.ANY)
    small = pltpu.VMEM((N_GX, 4, BP), F32)
    grid = pltpu.VMEM((BP, FULL), F32)
    lines = pltpu.VMEM((N_GX, 16, BP), F32)
    carries = pltpu.VMEM((N_GY, 8, BP), F32)
    out = pl.pallas_call(
        body,
        out_shape=jax.ShapeDtypeStruct((16, BP), F32),
        in_specs=[vmem, vmem, pl.BlockSpec(memory_space=pltpu.SMEM)] + [vmem] * 4 + [anywhere] * 8,
        out_specs=vmem,
        scratch_shapes=[
            pltpu.VMEM((NC, CP * BP), F32),
            pltpu.VMEM((NC, CP * CP), F32),
            pltpu.VMEM((2, FULL, FULL), BF16),
            pltpu.VMEM((2, FULL, FULL), BF16),
            pltpu.VMEM((16, FULL), F32),
            pltpu.VMEM((16, FULL), F32),
            pltpu.VMEM((BP, 4 * BP), BF16),
            pltpu.VMEM((4 * BP, BP), BF16),
            pltpu.VMEM((NC, BP), F32),
            small,
            small,
            grid,
            grid,
            lines,
            lines,
            carries,
            carries,
            carries,
            carries,
            lines,
            lines,
            grid,
            grid,
            small,
            small,
            pltpu.SemaphoreType.DMA((8,)),
            pltpu.SemaphoreType.DMA((8,)),
            pltpu.SemaphoreType.DMA((8,)),
        ],
        compiler_params=pltpu.CompilerParams(
            collective_id=0, has_side_effects=True, vmem_limit_bytes=48 * 1024 * 1024
        ),
    )(
        charges.reshape(16, BP),
        regions.reshape(16, BP),
        inv_permittivity,
        slab_owner.reshape(1, NC),
        brick_index.reshape(1, NC),
        near_target.reshape(1, NC),
        near_source.reshape(1, NC),
        projection,
        near_tiles,
        hx,
        hy,
        decay,
        gain,
        spread,
        gather,
    )
    return out.reshape(-1)


def solution(mesh):
    both = P(("gx", "gy"))
    wide = P(("gx", "gy"), None)
    return jax.shard_map(
        on_device,
        mesh=mesh,
        in_specs=(both, both, P(), wide, both, both, wide, both, both),
        out_specs=both,
        check_vma=False,
    )
```

```python
import functools
import math

import jax
import jax.numpy as jnp
import numpy as np
from jax import lax
from jax.experimental import pallas as pl
from jax.experimental.pallas import tpu as pltpu
from jax.sharding import PartitionSpec as P

CP = 64
NREG = 8
N_GX = 32
N_GY = 16
NC = 32
BP = 128
FULL = 512
G3 = 256
ZC = 128
SCREENING = 0.001
GROUPS = 4
PER_GROUP = N_GX // GROUPS
SLOTS = PER_GROUP * NC

F32 = jnp.float32
BF16 = jnp.bfloat16
HIGHEST = lax.Precision.HIGHEST
MESH = pl.DeviceIdType.MESH

NN = (((1,), (0,)), ((), ()))
NT = (((1,), (1,)), ((), ()))


@functools.lru_cache(maxsize=None)
def host_tables():
    def halves(table):
        table = table.astype(np.float32)
        high = table.astype(BF16)
        low = (table - high.astype(np.float32)).astype(BF16)
        return np.stack([high, low])

    def modes(length):
        n = np.arange(length)
        angle = (n[:, None] * n[None, :] % length) * (2.0 * math.pi / length)
        return np.cos(angle) + np.sin(angle)

    gy, dy, by = np.meshgrid(np.arange(N_GY), np.arange(4), np.arange(8), indexing="ij")
    along_y = modes(FULL)[(gy * 32 + by * 4 + dy).reshape(-1)]
    along_z = modes(G3)[:, :ZC]
    kx = np.repeat(np.arange(FULL).reshape(N_GX, 16), 8, axis=1)
    place = np.arange(128)
    angle = (kx[:, None, :] * 4 * place[None, :, None] % FULL) * (2.0 * math.pi / FULL)
    phases = halves(np.concatenate([np.cos(angle), np.sin(angle)], axis=2)).transpose(1, 0, 2, 3)
    dx = np.arange(4)
    angle = kx[:, None, :] * dx[None, :, None] * (2.0 * math.pi / FULL)
    planes = np.concatenate([np.cos(angle) + np.sin(angle), np.cos(angle) - np.sin(angle)], axis=1)
    squares = 4.0 * np.sin(np.arange(FULL) * (math.pi / FULL)) ** 2
    deep = 4.0 * np.sin(np.arange(G3) * (math.pi / G3)) ** 2 + SCREENING
    return (
        halves(along_y),
        halves(along_z),
        halves(along_z.T),
        phases,
        planes.astype(np.float32),
        np.broadcast_to(squares[:, None, None], (FULL, 1, BP)).astype(np.float32),
        squares[None, :].astype(np.float32),
        np.broadcast_to(deep[:, None], (G3, BP)).astype(np.float32),
    )


def halves(value):
    high = value.astype(BF16)
    return high, (value - high.astype(F32)).astype(BF16)


def dot(left, right, dims):
    return lax.dot_general(left, right, dims, preferred_element_type=F32)


def product(left, right, dims):
    return dot(left[0], right[0], dims) + dot(left[0], right[1], dims) + dot(left[1], right[0], dims)


def lanes(shape):
    return lax.broadcasted_iota(jnp.int32, shape, 1)


def rows(shape):
    return lax.broadcasted_iota(jnp.int32, shape, 0)


def lane_sums(leaf, first, count):
    if count == 1:
        return leaf(first)
    half = count // 2
    left = lane_sums(leaf, first, half)
    right = lane_sums(leaf, first + half, half)
    upper = (lanes(left.shape) & half) != 0
    return jnp.where(upper, right, left) + pltpu.roll(
        jnp.where(upper, left, right), 128 - half, 1
    )


def swap_blocks(parts):
    parts = list(parts)
    block = lanes(parts[0].shape) // 8
    for bit in (8, 4, 2, 1):
        upper = (block & bit) != 0
        for i in range(16):
            if i & bit:
                continue
            a, b = parts[i], parts[i | bit]
            parts[i] = jnp.where(upper, pltpu.roll(b, 8 * bit, 1), a)
            parts[i | bit] = jnp.where(upper, b, pltpu.roll(a, 128 - 8 * bit, 1))
    return parts


def far_first(step, half):
    return half + (1 - 2 * (step % 2)) * ((step + 1) // 2)


def gx_offset(me, slot, sign):
    dx, dz = far_first(slot // 8, 2), far_first(slot % 8, 4)
    x = lax.rem(me // 8 + sign * dx + 4, 4)
    z = lax.rem(me % 8 + sign * dz + 8, 8)
    return x * 8 + z


def send_slots(first, last, me, sign, source, target, send_sem, recv_sem):
    def step(slot, carry):
        pltpu.make_async_remote_copy(
            src_ref=source(slot),
            dst_ref=target(slot),
            send_sem=send_sem,
            recv_sem=recv_sem,
            device_id={"gx": gx_offset(me, slot, sign)},
            device_id_type=MESH,
        ).start()
        return carry

    lax.fori_loop(first, last, step, 0)


def send_columns(me, source, target, send_sem, recv_sem):
    def step(i, carry):
        other = lax.rem(me + far_first(i, 8), N_GY)
        pltpu.make_async_remote_copy(
            src_ref=source.at[other],
            dst_ref=target.at[me],
            send_sem=send_sem,
            recv_sem=recv_sem,
            device_id={"gy": other},
            device_id_type=MESH,
        ).start()
        return carry

    lax.fori_loop(0, N_GY - 1, step, 0)
    target[me] = source[me]


def wait_for(part, sem):
    pltpu.make_async_copy(part, part, sem).wait()


def body(
    charges_hbm,
    regions_hbm,
    inv_hbm,
    owner_hbm,
    index_hbm,
    target_hbm,
    source_hbm,
    projection_hbm,
    tiles_hbm,
    hy_hbm,
    hz_hbm,
    hzt_hbm,
    phases_hbm,
    planes_hbm,
    along_x_hbm,
    along_y_hbm,
    along_z_hbm,
    out_ref,
    charges_ref,
    regions_ref,
    inv_ref,
    owner_ref,
    index_ref,
    target_ref,
    source_ref,
    projection_ref,
    tiles_ref,
    hy_ref,
    hz_ref,
    hzt_ref,
    phases_ref,
    planes_ref,
    along_x_ref,
    along_y_ref,
    along_z_ref,
    rows_ref,
    near_ref,
    kernel_ref,
    turn_ref,
    cells_ref,
    spread_ref,
    grid_ref,
    send_i,
    recv_i,
    send_b,
    recv_b,
    send_g,
    recv_g,
    send_f,
    recv_f,
    send_q,
    recv_q,
    local_sem,
    send_sem,
    recv_sem,
):
    gx = lax.axis_index("gx")
    gy = lax.axis_index("gy")
    sources = [
        owner_hbm,
        index_hbm,
        inv_hbm,
        regions_hbm,
        charges_hbm,
        projection_hbm,
        target_hbm,
        source_hbm,
        tiles_hbm,
        phases_hbm.at[gx],
        planes_hbm.at[gx],
        along_x_hbm.at[gx * 16 + gy],
        along_y_hbm,
        along_z_hbm,
        hy_hbm,
        hz_hbm,
        hzt_hbm,
    ]
    places = [
        owner_ref,
        index_ref,
        inv_ref,
        regions_ref,
        charges_ref,
        projection_ref,
        target_ref,
        source_ref,
        tiles_ref,
        phases_ref,
        planes_ref,
        along_x_ref,
        along_y_ref,
        along_z_ref,
        hy_ref,
        hz_ref,
        hzt_ref,
    ]
    loads = [
        pltpu.make_async_copy(source, place, local_sem.at[i])
        for i, (source, place) in enumerate(zip(sources, places))
    ]
    for load in loads:
        load.start()

    barrier = pltpu.get_barrier_semaphore()

    def greet(axis, me, count):
        def step(i, carry):
            pl.semaphore_signal(
                barrier, inc=1, device_id={axis: lax.rem(me + i, count)}, device_id_type=MESH
            )
            return carry

        lax.fori_loop(1, count, step, 0)

    greet("gx", gx, N_GX)
    greet("gy", gy, N_GY)

    for load in loads[0:2]:
        load.wait()
    brick = index_ref[...]
    place = (owner_ref[...] * 4 + (brick >> 7)) * 128 + (brick & 15) * 8 + ((brick >> 4) & 7)
    place = jnp.concatenate([place.astype(F32), jnp.zeros((1, BP - NC), F32)], axis=1)
    for v in range(4):
        send_i[v] = pltpu.roll(place, NC * v, 1) if v else place

    for load in loads[2:6]:
        load.wait()
    regions = regions_ref[...]
    factor = jnp.zeros(regions.shape, F32)
    for k in range(NREG):
        factor = jnp.where(regions == k, inv_ref[0:1, k : k + 1], factor)
    scaled = charges_ref[...] * factor
    rows_ref[pl.ds(0, 16, stride=2), :] = scaled
    rows_ref[pl.ds(1, 16, stride=2), :] = pltpu.roll(scaled, CP, 1)
    charge_rows = rows_ref[...]
    bricks = charge_rows[:, 0:1] * projection_ref[:, 0:BP]
    for p in range(1, CP):
        bricks = bricks + charge_rows[:, p : p + 1] * projection_ref[:, p * BP : (p + 1) * BP]
    send_b[...] = bricks

    pl.semaphore_wait(barrier, N_GX - 1 + N_GY - 1)
    last = N_GX - 1
    send_slots(
        0,
        last,
        gx,
        1,
        lambda s: send_i.at[s % 4],
        lambda s: recv_i.at[s],
        send_sem.at[0],
        recv_sem.at[0],
    )
    for g in range(GROUPS):
        send_slots(
            g * PER_GROUP,
            min((g + 1) * PER_GROUP, last),
            gx,
            1,
            lambda s: send_b,
            lambda s: recv_b.at[s],
            send_sem.at[1],
            recv_sem.at[1 + g],
        )
    recv_i[last] = send_i[last % 4]
    recv_b[last] = bricks

    for load in loads[6:9]:
        load.wait()
    shape = (NC, NC)
    eye = rows(shape) == lanes(shape)
    source_col = jnp.sum(
        jnp.where(eye, source_ref[...].astype(F32), 0.0), axis=1, keepdims=True
    )
    from_source = jnp.where(source_col == lanes(shape).astype(F32), 1.0, 0.0)
    near_charges = lax.dot_general(
        from_source, charge_rows, NN, precision=HIGHEST, preferred_element_type=F32
    )
    lower = lanes((NC, BP)) < CP
    near_charges = jnp.where(lower, near_charges, pltpu.roll(near_charges, CP, 1))

    def near_part(p):
        part = tiles_ref[:, p // 2 * BP : (p // 2 + 1) * BP] * near_charges
        return jnp.where(lower if p % 2 == 0 else jnp.logical_not(lower), part, 0.0)

    contrib = lane_sums(near_part, 0, CP)
    contrib = contrib + pltpu.roll(contrib, CP, 1)
    to_target = jnp.where(rows(shape) == target_ref[...], 1.0, 0.0)
    near_ref[...] = lax.dot_general(
        to_target, contrib, NN, precision=HIGHEST, preferred_element_type=F32
    )

    for load in loads[9:14]:
        load.wait()
    block = (NC, 4 * BP)
    point, lane = rows(block), lanes(block)
    keep = (point // 8 == lane // 128) & (point % 8 == lane % 8)
    for dx in range(4):
        for part in range(2):
            spread_ref[dx * NC : (dx + 1) * NC, part * FULL : (part + 1) * FULL] = jnp.where(
                keep,
                jnp.concatenate([planes_ref[part * 4 + dx : part * 4 + dx + 1, :]] * 4, axis=1),
                0.0,
            )
    spread = halves(spread_ref[...])

    for c in range(4):
        part = slice(c * 128, (c + 1) * 128)
        kernel_ref[:, part] = (1.0 / (FULL * FULL * G3)) / (
            along_x_ref[...] + along_y_ref[:, part] + along_z_ref[...]
        )

    wait_for(recv_i.at[0:last], recv_sem.at[0])
    for t in range(N_GX // 4):
        where = recv_i[4 * t]
        for v in range(1, 4):
            where = where + recv_i[4 * t + v]
        where = where.astype(jnp.int32)
        tile = rows((128, 128))
        cells_ref[:, t * 128 : (t + 1) * 128] = jnp.where((where & 127) == tile, 1.0, 0.0)
        at_plane = jnp.where((where >> 7) == tile, 1.0, 0.0).T.astype(BF16)
        turn_ref[t * 128 : (t + 1) * 128, :] = dot(at_plane, phases_ref[0], NN) + dot(
            at_plane, phases_ref[1], NN
        )

    grid = None
    for g in range(GROUPS):
        begin, end = g * PER_GROUP, (g + 1) * PER_GROUP
        wait_for(recv_b.at[begin : min(end, last)], recv_sem.at[1 + g])
        values = halves(recv_b[begin:end].reshape(SLOTS, BP))
        parts = product(values, spread, NN)
        turn = turn_ref[g * SLOTS : (g + 1) * SLOTS, :]
        cosine = jnp.concatenate([turn[:, 0:BP]] * 4, axis=1)
        sine = jnp.concatenate([turn[:, BP : 2 * BP]] * 4, axis=1)
        placed = halves(cosine * parts[:, 0:FULL] + sine * parts[:, FULL : 2 * FULL])
        cells = cells_ref[:, g * SLOTS : (g + 1) * SLOTS].astype(BF16)
        term = dot(cells, placed[0], NN) + dot(cells, placed[1], NN)
        grid = term if grid is None else grid + term
    grid_ref[...] = grid
    for d in range(4):
        parts = swap_blocks([grid_ref[b * 8 : (b + 1) * 8, d * BP : (d + 1) * BP] for b in range(16)])
        for k in range(16):
            send_g[k, d * 8 : (d + 1) * 8, :] = parts[k]
    send_columns(gy, send_g, recv_g, send_sem.at[2], recv_sem.at[5])

    for load in loads[14:17]:
        load.wait()
    wait_for(recv_g.at[0 : N_GY - 1], recv_sem.at[5])
    turned = recv_g[...].reshape(FULL, ZC).T
    hy = (hy_ref[0], hy_ref[1])
    field = product(halves(turned), hy, NN)
    field = product((hz_ref[0], hz_ref[1]), halves(field), NN) * kernel_ref[...]
    field = product((hzt_ref[0], hzt_ref[1]), halves(field), NN)
    send_f[...] = product(hy, halves(field), NT).reshape(N_GY, 32, ZC)
    send_columns(gy, send_f, recv_f, send_sem.at[3], recv_sem.at[6])
    wait_for(recv_f.at[0 : N_GY - 1], recv_sem.at[6])

    for d in range(4):
        parts = swap_blocks([recv_f[k, d * 8 : (d + 1) * 8, :] for k in range(16)])
        for b in range(16):
            grid_ref[b * 8 : (b + 1) * 8, d * BP : (d + 1) * BP] = parts[b]
    field = halves(grid_ref[...])
    for g in range(GROUPS):
        begin, end = g * PER_GROUP, (g + 1) * PER_GROUP
        cells = cells_ref[:, g * SLOTS : (g + 1) * SLOTS].T.astype(BF16)
        lines = dot(cells, field[0], NN) + dot(cells, field[1], NN)
        turn = turn_ref[g * SLOTS : (g + 1) * SLOTS, :]
        cosine = jnp.concatenate([turn[:, 0:BP]] * 4, axis=1)
        sine = jnp.concatenate([turn[:, BP : 2 * BP]] * 4, axis=1)
        lines = halves(jnp.concatenate([cosine * lines, sine * lines], axis=1))
        send_q[begin:end] = product(lines, spread, NT).reshape(PER_GROUP, NC, BP)
        send_slots(
            begin,
            min(end, last),
            gx,
            -1,
            lambda s: send_q.at[s],
            lambda s: recv_q.at[s],
            send_sem.at[4],
            recv_sem.at[7],
        )
    samples = send_q[last]
    wait_for(recv_q.at[0:last], recv_sem.at[7])
    for s in range(last):
        samples = samples + recv_q[s]

    def far_part(p):
        return projection_ref[:, p * BP : (p + 1) * BP] * samples

    far_field = lane_sums(far_part, 0, CP)
    far_field = far_field + pltpu.roll(far_field, CP, 1)
    rows_ref[...] = far_field + near_ref[...]
    even = rows_ref[pl.ds(0, 16, stride=2), :]
    odd = rows_ref[pl.ds(1, 16, stride=2), :]
    out_ref[...] = jnp.where(lanes((16, BP)) < CP, even, pltpu.roll(odd, CP, 1))

    wait_for(recv_i.at[0:last], send_sem.at[0])
    wait_for(recv_b.at[0:last], send_sem.at[1])
    wait_for(send_g.at[0 : N_GY - 1], send_sem.at[2])
    wait_for(send_f.at[0 : N_GY - 1], send_sem.at[3])
    wait_for(send_q.at[0:last], send_sem.at[4])


def on_device(
    charges,
    regions,
    inv_permittivity,
    projection,
    slab_owner,
    brick_index,
    near_tiles,
    near_target,
    near_source,
):
    tables = [jnp.asarray(t) for t in host_tables()]
    in_hbm = pl.BlockSpec(memory_space=pltpu.HBM)
    small = pltpu.VMEM((1, NC), jnp.int32)
    bricks = pltpu.VMEM((N_GX, NC, BP), F32)
    columns = pltpu.VMEM((N_GY, 32, ZC), F32)
    out = pl.pallas_call(
        body,
        out_shape=jax.ShapeDtypeStruct((16, BP), F32),
        in_specs=[in_hbm] * 17,
        out_specs=pl.BlockSpec(memory_space=pltpu.VMEM),
        scratch_shapes=[
            pltpu.VMEM((16, BP), F32),
            pltpu.VMEM((16, BP), jnp.int32),
            pltpu.VMEM((1, NREG), F32),
            small,
            small,
            small,
            small,
            pltpu.VMEM((NC, CP * BP), F32),
            pltpu.VMEM((NC, CP * CP), F32),
            pltpu.VMEM((2, FULL, FULL), BF16),
            pltpu.VMEM((2, G3, ZC), BF16),
            pltpu.VMEM((2, ZC, G3), BF16),
            pltpu.VMEM((2, 128, 2 * BP), BF16),
            pltpu.VMEM((8, BP), F32),
            pltpu.VMEM((1, BP), F32),
            pltpu.VMEM((1, FULL), F32),
            pltpu.VMEM((G3, BP), F32),
            pltpu.VMEM((NC, BP), F32),
            pltpu.VMEM((NC, BP), F32),
            pltpu.VMEM((G3, FULL), F32),
            pltpu.VMEM((N_GX * NC, 2 * BP), F32),
            pltpu.VMEM((128, N_GX * NC), F32),
            pltpu.VMEM((BP, 2 * FULL), F32),
            pltpu.VMEM((128, FULL), F32),
            pltpu.VMEM((4, 1, BP), F32),
            pltpu.VMEM((N_GX, 1, BP), F32),
            pltpu.VMEM((NC, BP), F32),
            bricks,
            columns,
            columns,
            columns,
            columns,
            bricks,
            bricks,
            pltpu.SemaphoreType.DMA((17,)),
            pltpu.SemaphoreType.DMA((5,)),
            pltpu.SemaphoreType.DMA((8,)),
        ],
        compiler_params=pltpu.CompilerParams(
            collective_id=0, has_side_effects=True, vmem_limit_bytes=60 * 1024 * 1024
        ),
    )(
        charges.reshape(16, BP),
        regions.reshape(16, BP),
        inv_permittivity.reshape(1, NREG),
        slab_owner.reshape(1, NC),
        brick_index.reshape(1, NC),
        near_target.reshape(1, NC),
        near_source.reshape(1, NC),
        projection,
        near_tiles,
        *tables,
    )
    return out.reshape(-1)


def solution(mesh):
    both = P(("gx", "gy"))
    wide = P(("gx", "gy"), None)
    return jax.shard_map(
        on_device,
        mesh=mesh,
        in_specs=(both, both, P(), wide, both, both, wide, both, both),
        out_specs=both,
        check_vma=False,
    )
```

```python
import functools
import math

import jax
import jax.numpy as jnp
import numpy as np
from jax import lax
from jax.experimental import pallas as pl
from jax.experimental.pallas import tpu as pltpu
from jax.sharding import PartitionSpec as P

CP = 64
NREG = 8
N_GX = 32
N_GY = 16
N_X = 4
N_Z = 8
NC = 32
BP = 128
FULL = 512
G3 = 256
ZC = 128
SCREENING = 0.001
GROUPS = 4
PER_GROUP = N_GX // GROUPS
SLOTS = PER_GROUP * NC

F32 = jnp.float32
BF16 = jnp.bfloat16
HIGHEST = lax.Precision.HIGHEST
MESH = pl.DeviceIdType.MESH

NN = (((1,), (0,)), ((), ()))
NT = (((1,), (1,)), ((), ()))


@functools.lru_cache(maxsize=None)
def host_tables():
    def halves(table):
        table = table.astype(np.float32)
        high = table.astype(BF16)
        low = (table - high.astype(np.float32)).astype(BF16)
        return np.stack([high, low])

    def modes(length):
        n = np.arange(length)
        angle = (n[:, None] * n[None, :] % length) * (2.0 * math.pi / length)
        return np.cos(angle) + np.sin(angle)

    gy, dy, by = np.meshgrid(np.arange(N_GY), np.arange(4), np.arange(8), indexing="ij")
    along_y = modes(FULL)[(gy * 32 + by * 4 + dy).reshape(-1)]
    along_z = modes(G3)[:, :ZC]
    kx = np.repeat(np.arange(FULL).reshape(N_GX, 16), 8, axis=1)
    place = np.arange(128)
    angle = (kx[:, None, :] * 4 * place[None, :, None] % FULL) * (2.0 * math.pi / FULL)
    phases = halves(np.concatenate([np.cos(angle), np.sin(angle)], axis=2)).transpose(1, 0, 2, 3)
    dx = np.arange(4)
    angle = kx[:, None, :] * dx[None, :, None] * (2.0 * math.pi / FULL)
    planes = np.concatenate([np.cos(angle) + np.sin(angle), np.cos(angle) - np.sin(angle)], axis=1)
    squares = 4.0 * np.sin(np.arange(FULL) * (math.pi / FULL)) ** 2
    deep = 4.0 * np.sin(np.arange(G3) * (math.pi / G3)) ** 2 + SCREENING
    return (
        halves(along_y),
        halves(along_z),
        halves(along_z.T),
        phases,
        planes.astype(np.float32),
        np.broadcast_to(squares[:, None, None], (FULL, 1, BP)).astype(np.float32),
        squares[None, :].astype(np.float32),
        np.broadcast_to(deep[:, None], (G3, BP)).astype(np.float32),
    )


def halves(value):
    high = value.astype(BF16)
    return high, (value - high.astype(F32)).astype(BF16)


def dot(left, right, dims):
    return lax.dot_general(left, right, dims, preferred_element_type=F32)


def product(left, right, dims):
    return dot(left[0], right[0], dims) + dot(left[0], right[1], dims) + dot(left[1], right[0], dims)


def lanes(shape):
    return lax.broadcasted_iota(jnp.int32, shape, 1)


def rows(shape):
    return lax.broadcasted_iota(jnp.int32, shape, 0)


def lane_sums(leaf, first, count):
    if count == 1:
        return leaf(first)
    half = count // 2
    left = lane_sums(leaf, first, half)
    right = lane_sums(leaf, first + half, half)
    upper = (lanes(left.shape) & half) != 0
    return jnp.where(upper, right, left) + pltpu.roll(
        jnp.where(upper, left, right), 128 - half, 1
    )


def swap_blocks(parts):
    parts = list(parts)
    block = lanes(parts[0].shape) // 8
    for bit in (8, 4, 2, 1):
        upper = (block & bit) != 0
        for i in range(16):
            if i & bit:
                continue
            a, b = parts[i], parts[i | bit]
            parts[i] = jnp.where(upper, pltpu.roll(b, 8 * bit, 1), a)
            parts[i | bit] = jnp.where(upper, b, pltpu.roll(a, 128 - 8 * bit, 1))
    return parts


def far_first(step, half):
    return half + (1 - 2 * (step % 2)) * ((step + 1) // 2)


def remote(source, target, axis, other, send_sem, recv_sem):
    pltpu.make_async_remote_copy(
        src_ref=source,
        dst_ref=target,
        send_sem=send_sem,
        recv_sem=recv_sem,
        device_id={axis: other},
        device_id_type=MESH,
    ).start()


def loop(count, step):
    def one(i, carry):
        step(i)
        return carry

    lax.fori_loop(0, count, one, 0)


def on_z(me, j, sign):
    return me // 8 * 8 + lax.rem(me % 8 + sign * far_first(j, 4) + 8, 8)


def on_x(me, i, sign):
    return lax.rem(me // 8 + sign * far_first(i, 2) + 4, 4) * 8 + me % 8


def send_columns(me, source, target, send_sem, recv_sem):
    def step(i):
        other = lax.rem(me + far_first(i, 8), N_GY)
        remote(source.at[other], target.at[me], "gy", other, send_sem, recv_sem)

    loop(N_GY - 1, step)
    target[me] = source[me]


def wait_for(part, sem):
    pltpu.make_async_copy(part, part, sem).wait()


def body(
    charges_hbm,
    regions_hbm,
    inv_hbm,
    owner_hbm,
    index_hbm,
    target_hbm,
    source_hbm,
    projection_hbm,
    tiles_hbm,
    hy_hbm,
    hz_hbm,
    hzt_hbm,
    phases_hbm,
    planes_hbm,
    along_x_hbm,
    along_y_hbm,
    along_z_hbm,
    out_ref,
    charges_ref,
    regions_ref,
    inv_ref,
    owner_ref,
    index_ref,
    target_ref,
    source_ref,
    projection_ref,
    tiles_ref,
    hy_ref,
    hz_ref,
    hzt_ref,
    phases_ref,
    planes_ref,
    along_x_ref,
    along_y_ref,
    along_z_ref,
    rows_ref,
    near_ref,
    kernel_ref,
    turn_ref,
    cells_ref,
    spread_ref,
    grid_ref,
    send_i,
    recv_i,
    send_b,
    recv_b,
    send_g,
    recv_g,
    send_f,
    recv_f,
    send_q,
    recv_q,
    send_r,
    recv_r,
    local_sem,
    send_sem,
    recv_sem,
    ring_sem,
    line_sem,
    back_sem,
):
    gx = lax.axis_index("gx")
    gy = lax.axis_index("gy")
    sources = [
        owner_hbm,
        index_hbm,
        inv_hbm,
        regions_hbm,
        charges_hbm,
        projection_hbm,
        target_hbm,
        source_hbm,
        tiles_hbm,
        phases_hbm.at[gx],
        planes_hbm.at[gx],
        along_x_hbm.at[gx * 16 + gy],
        along_y_hbm,
        along_z_hbm,
        hy_hbm,
        hz_hbm,
        hzt_hbm,
    ]
    places = [
        owner_ref,
        index_ref,
        inv_ref,
        regions_ref,
        charges_ref,
        projection_ref,
        target_ref,
        source_ref,
        tiles_ref,
        phases_ref,
        planes_ref,
        along_x_ref,
        along_y_ref,
        along_z_ref,
        hy_ref,
        hz_ref,
        hzt_ref,
    ]
    loads = [
        pltpu.make_async_copy(source, place, local_sem.at[i])
        for i, (source, place) in enumerate(zip(sources, places))
    ]
    for load in loads:
        load.start()

    barrier = pltpu.get_barrier_semaphore()

    def greet(axis, other):
        pl.semaphore_signal(barrier, inc=1, device_id={axis: other}, device_id_type=MESH)

    loop(N_Z - 1, lambda j: greet("gx", on_z(gx, j, 1)))
    loop(N_GY - 1, lambda i: greet("gy", lax.rem(gy + far_first(i, 8), N_GY)))
    loop(N_X - 1, lambda i: greet("gx", on_x(gx, i, 1)))

    for load in loads[0:2]:
        load.wait()
    brick = index_ref[...]
    place = (owner_ref[...] * 4 + (brick >> 7)) * 128 + (brick & 15) * 8 + ((brick >> 4) & 7)
    place = jnp.concatenate([place.astype(F32), jnp.zeros((1, BP - NC), F32)], axis=1)
    for v in range(4):
        send_i[v] = pltpu.roll(place, NC * v, 1) if v else place

    for load in loads[2:6]:
        load.wait()
    regions = regions_ref[...]
    factor = jnp.zeros(regions.shape, F32)
    for k in range(NREG):
        factor = jnp.where(regions == k, inv_ref[0:1, k : k + 1], factor)
    scaled = charges_ref[...] * factor
    rows_ref[pl.ds(0, 16, stride=2), :] = scaled
    rows_ref[pl.ds(1, 16, stride=2), :] = pltpu.roll(scaled, CP, 1)
    charge_rows = rows_ref[...]
    bricks = charge_rows[:, 0:1] * projection_ref[:, 0:BP]
    for p in range(1, CP):
        bricks = bricks + charge_rows[:, p : p + 1] * projection_ref[:, p * BP : (p + 1) * BP]
    send_b[...] = bricks

    pl.semaphore_wait(barrier, N_Z - 1 + N_X - 1 + N_GY - 1)
    last = N_GX - 1
    ring = N_Z - 1
    base = N_GX - N_Z

    def to_ring(j):
        other = on_z(gx, j, 1)
        remote(send_i.at[j % 4], recv_i.at[base + j], "gx", other, send_sem.at[0], ring_sem.at[0, j])
        remote(send_b, recv_b.at[base + j], "gx", other, send_sem.at[1], ring_sem.at[1, j])

    loop(ring, to_ring)
    recv_i[last] = send_i[last % 4]
    recv_b[last] = bricks

    def to_line(index, block, j):
        for i in range(N_X - 1):
            other = on_x(gx, i, 1)
            remote(index, recv_i.at[i * N_Z + j], "gx", other, send_sem.at[2], line_sem.at[i, 0])
            remote(block, recv_b.at[i * N_Z + j], "gx", other, send_sem.at[3], line_sem.at[i, 1])

    to_line(send_i.at[last % 4], send_b, ring)

    for load in loads[6:9]:
        load.wait()
    shape = (NC, NC)
    eye = rows(shape) == lanes(shape)
    source_col = jnp.sum(
        jnp.where(eye, source_ref[...].astype(F32), 0.0), axis=1, keepdims=True
    )
    from_source = jnp.where(source_col == lanes(shape).astype(F32), 1.0, 0.0)
    near_charges = lax.dot_general(
        from_source, charge_rows, NN, precision=HIGHEST, preferred_element_type=F32
    )
    lower = lanes((NC, BP)) < CP
    near_charges = jnp.where(lower, near_charges, pltpu.roll(near_charges, CP, 1))

    def near_part(p):
        part = tiles_ref[:, p // 2 * BP : (p // 2 + 1) * BP] * near_charges
        return jnp.where(lower if p % 2 == 0 else jnp.logical_not(lower), part, 0.0)

    contrib = lane_sums(near_part, 0, CP)
    contrib = contrib + pltpu.roll(contrib, CP, 1)
    to_target = jnp.where(rows(shape) == target_ref[...], 1.0, 0.0)
    near_ref[...] = lax.dot_general(
        to_target, contrib, NN, precision=HIGHEST, preferred_element_type=F32
    )

    for load in loads[9:14]:
        load.wait()
    block = (NC, 4 * BP)
    point, lane = rows(block), lanes(block)
    keep = (point // 8 == lane // 128) & (point % 8 == lane % 8)
    for dx in range(4):
        for part in range(2):
            spread_ref[dx * NC : (dx + 1) * NC, part * FULL : (part + 1) * FULL] = jnp.where(
                keep,
                jnp.concatenate([planes_ref[part * 4 + dx : part * 4 + dx + 1, :]] * 4, axis=1),
                0.0,
            )
    spread = halves(spread_ref[...])

    for c in range(4):
        part = slice(c * 128, (c + 1) * 128)
        kernel_ref[:, part] = (1.0 / (FULL * FULL * G3)) / (
            along_x_ref[...] + along_y_ref[:, part] + along_z_ref[...]
        )

    def pass_on(step):
        j = ring - 1 - step
        wait_for(recv_i.at[base + j], ring_sem.at[0, j])
        wait_for(recv_b.at[base + j], ring_sem.at[1, j])
        to_line(recv_i.at[base + j], recv_b.at[base + j], j)

    loop(ring, pass_on)

    for i in range(N_X - 1):
        wait_for(recv_i.at[i * N_Z : (i + 1) * N_Z], line_sem.at[i, 0])
    for t in range(N_GX // 4):
        where = recv_i[4 * t]
        for v in range(1, 4):
            where = where + recv_i[4 * t + v]
        where = where.astype(jnp.int32)
        tile = rows((128, 128))
        cells_ref[:, t * 128 : (t + 1) * 128] = jnp.where((where & 127) == tile, 1.0, 0.0)
        at_plane = jnp.where((where >> 7) == tile, 1.0, 0.0).T.astype(BF16)
        turn_ref[t * 128 : (t + 1) * 128, :] = dot(at_plane, phases_ref[0], NN) + dot(
            at_plane, phases_ref[1], NN
        )

    grid = None
    for g in (3, 1, 2, 0):
        begin, end = g * PER_GROUP, (g + 1) * PER_GROUP
        if g < N_X - 1:
            wait_for(recv_b.at[begin:end], line_sem.at[g, 1])
        values = halves(recv_b[begin:end].reshape(SLOTS, BP))
        parts = product(values, spread, NN)
        turn = turn_ref[g * SLOTS : (g + 1) * SLOTS, :]
        cosine = jnp.concatenate([turn[:, 0:BP]] * 4, axis=1)
        sine = jnp.concatenate([turn[:, BP : 2 * BP]] * 4, axis=1)
        placed = halves(cosine * parts[:, 0:FULL] + sine * parts[:, FULL : 2 * FULL])
        cells = cells_ref[:, g * SLOTS : (g + 1) * SLOTS].astype(BF16)
        term = dot(cells, placed[0], NN) + dot(cells, placed[1], NN)
        grid = term if grid is None else grid + term
    grid_ref[...] = grid
    for d in range(4):
        parts = swap_blocks([grid_ref[b * 8 : (b + 1) * 8, d * BP : (d + 1) * BP] for b in range(16)])
        for k in range(16):
            send_g[k, d * 8 : (d + 1) * 8, :] = parts[k]
    send_columns(gy, send_g, recv_g, send_sem.at[4], recv_sem.at[0])

    for load in loads[14:17]:
        load.wait()
    wait_for(recv_g.at[0 : N_GY - 1], recv_sem.at[0])
    turned = recv_g[...].reshape(FULL, ZC).T
    hy = (hy_ref[0], hy_ref[1])
    field = product(halves(turned), hy, NN)
    field = product((hz_ref[0], hz_ref[1]), halves(field), NN) * kernel_ref[...]
    field = product((hzt_ref[0], hzt_ref[1]), halves(field), NN)
    send_f[...] = product(hy, halves(field), NT).reshape(N_GY, 32, ZC)
    send_columns(gy, send_f, recv_f, send_sem.at[5], recv_sem.at[1])
    wait_for(recv_f.at[0 : N_GY - 1], recv_sem.at[1])

    for d in range(4):
        parts = swap_blocks([recv_f[k, d * 8 : (d + 1) * 8, :] for k in range(16)])
        for b in range(16):
            grid_ref[b * 8 : (b + 1) * 8, d * BP : (d + 1) * BP] = parts[b]
    field = halves(grid_ref[...])
    for g in range(GROUPS):
        begin, end = g * PER_GROUP, (g + 1) * PER_GROUP
        cells = cells_ref[:, g * SLOTS : (g + 1) * SLOTS].T.astype(BF16)
        lines = dot(cells, field[0], NN) + dot(cells, field[1], NN)
        turn = turn_ref[g * SLOTS : (g + 1) * SLOTS, :]
        cosine = jnp.concatenate([turn[:, 0:BP]] * 4, axis=1)
        sine = jnp.concatenate([turn[:, BP : 2 * BP]] * 4, axis=1)
        lines = halves(jnp.concatenate([cosine * lines, sine * lines], axis=1))
        send_q[begin:end] = product(lines, spread, NT).reshape(PER_GROUP, NC, BP)
        if g < N_X - 1:

            def back_on_line(j, g=g):
                slot = g * N_Z + j
                remote(
                    send_q.at[slot],
                    recv_q.at[j, g],
                    "gx",
                    on_x(gx, g, -1),
                    send_sem.at[6],
                    back_sem.at[j],
                )

            loop(N_Z, back_on_line)

    def add_line(j):
        wait_for(recv_q.at[j], back_sem.at[j])
        return send_q[base + j] + recv_q[j, 0] + recv_q[j, 1] + recv_q[j, 2]

    def back_on_ring(j):
        send_r[j] = add_line(j)
        remote(send_r.at[j], recv_r.at[j], "gx", on_z(gx, j, -1), send_sem.at[7], recv_sem.at[2])

    loop(ring, back_on_ring)
    samples = add_line(ring)
    wait_for(recv_r.at[0:ring], recv_sem.at[2])
    for j in range(ring):
        samples = samples + recv_r[j]

    def far_part(p):
        return projection_ref[:, p * BP : (p + 1) * BP] * samples

    far_field = lane_sums(far_part, 0, CP)
    far_field = far_field + pltpu.roll(far_field, CP, 1)
    rows_ref[...] = far_field + near_ref[...]
    even = rows_ref[pl.ds(0, 16, stride=2), :]
    odd = rows_ref[pl.ds(1, 16, stride=2), :]
    out_ref[...] = jnp.where(lanes((16, BP)) < CP, even, pltpu.roll(odd, CP, 1))

    wait_for(recv_i.at[0:ring], send_sem.at[0])
    wait_for(recv_b.at[0:ring], send_sem.at[1])
    wait_for(recv_i.at[0:base], send_sem.at[2])
    wait_for(recv_b.at[0:base], send_sem.at[3])
    wait_for(send_g.at[0 : N_GY - 1], send_sem.at[4])
    wait_for(send_f.at[0 : N_GY - 1], send_sem.at[5])
    wait_for(send_q.at[0:base], send_sem.at[6])
    wait_for(send_r.at[0:ring], send_sem.at[7])


def on_device(
    charges,
    regions,
    inv_permittivity,
    projection,
    slab_owner,
    brick_index,
    near_tiles,
    near_target,
    near_source,
):
    tables = [jnp.asarray(t) for t in host_tables()]
    in_hbm = pl.BlockSpec(memory_space=pltpu.HBM)
    small = pltpu.VMEM((1, NC), jnp.int32)
    bricks = pltpu.VMEM((N_GX, NC, BP), F32)
    columns = pltpu.VMEM((N_GY, 32, ZC), F32)
    out = pl.pallas_call(
        body,
        out_shape=jax.ShapeDtypeStruct((16, BP), F32),
        in_specs=[in_hbm] * 17,
        out_specs=pl.BlockSpec(memory_space=pltpu.VMEM),
        scratch_shapes=[
            pltpu.VMEM((16, BP), F32),
            pltpu.VMEM((16, BP), jnp.int32),
            pltpu.VMEM((1, NREG), F32),
            small,
            small,
            small,
            small,
            pltpu.VMEM((NC, CP * BP), F32),
            pltpu.VMEM((NC, CP * CP), F32),
            pltpu.VMEM((2, FULL, FULL), BF16),
            pltpu.VMEM((2, G3, ZC), BF16),
            pltpu.VMEM((2, ZC, G3), BF16),
            pltpu.VMEM((2, 128, 2 * BP), BF16),
            pltpu.VMEM((8, BP), F32),
            pltpu.VMEM((1, BP), F32),
            pltpu.VMEM((1, FULL), F32),
            pltpu.VMEM((G3, BP), F32),
            pltpu.VMEM((NC, BP), F32),
            pltpu.VMEM((NC, BP), F32),
            pltpu.VMEM((G3, FULL), F32),
            pltpu.VMEM((N_GX * NC, 2 * BP), F32),
            pltpu.VMEM((128, N_GX * NC), F32),
            pltpu.VMEM((BP, 2 * FULL), F32),
            pltpu.VMEM((128, FULL), F32),
            pltpu.VMEM((4, 1, BP), F32),
            pltpu.VMEM((N_GX, 1, BP), F32),
            pltpu.VMEM((NC, BP), F32),
            bricks,
            columns,
            columns,
            columns,
            columns,
            bricks,
            pltpu.VMEM((N_Z, N_X - 1, NC, BP), F32),
            pltpu.VMEM((N_Z - 1, NC, BP), F32),
            pltpu.VMEM((N_Z - 1, NC, BP), F32),
            pltpu.SemaphoreType.DMA((17,)),
            pltpu.SemaphoreType.DMA((8,)),
            pltpu.SemaphoreType.DMA((3,)),
            pltpu.SemaphoreType.DMA((2, N_Z - 1)),
            pltpu.SemaphoreType.DMA((N_X - 1, 2)),
            pltpu.SemaphoreType.DMA((N_Z,)),
        ],
        compiler_params=pltpu.CompilerParams(
            collective_id=0, has_side_effects=True, vmem_limit_bytes=60 * 1024 * 1024
        ),
    )(
        charges.reshape(16, BP),
        regions.reshape(16, BP),
        inv_permittivity.reshape(1, NREG),
        slab_owner.reshape(1, NC),
        brick_index.reshape(1, NC),
        near_target.reshape(1, NC),
        near_source.reshape(1, NC),
        projection,
        near_tiles,
        *tables,
    )
    return out.reshape(-1)


def solution(mesh):
    both = P(("gx", "gy"))
    wide = P(("gx", "gy"), None)
    return jax.shard_map(
        on_device,
        mesh=mesh,
        in_specs=(both, both, P(), wide, both, both, wide, both, both),
        out_specs=both,
        check_vma=False,
    )
```

```python
import functools
import math

import jax
import jax.numpy as jnp
import numpy as np
from jax import lax
from jax.experimental import pallas as pl
from jax.experimental.pallas import tpu as pltpu
from jax.sharding import PartitionSpec as P

CP = 64
NREG = 8
N_GX = 32
N_GY = 16
N_X = 4
N_Z = 8
NC = 32
BP = 128
FULL = 512
G3 = 256
ZC = 128
SCREENING = 0.001
Z_OFFSETS = (4, 3, 5, 2, 6, 1, 7, 0)
X_OFFSETS = (2, 1, 3, 0)
GROUPS = 4
PER_GROUP = N_GX // GROUPS
SLOTS = PER_GROUP * NC

F32 = jnp.float32
BF16 = jnp.bfloat16
HIGHEST = lax.Precision.HIGHEST
MESH = pl.DeviceIdType.MESH

NN = (((1,), (0,)), ((), ()))
NT = (((1,), (1,)), ((), ()))


@functools.lru_cache(maxsize=None)
def host_tables():
    def halves(table):
        table = table.astype(np.float32)
        high = table.astype(BF16)
        low = (table - high.astype(np.float32)).astype(BF16)
        return np.stack([high, low])

    def modes(length):
        n = np.arange(length)
        angle = (n[:, None] * n[None, :] % length) * (2.0 * math.pi / length)
        return np.cos(angle) + np.sin(angle)

    gy, dy, by = np.meshgrid(np.arange(N_GY), np.arange(4), np.arange(8), indexing="ij")
    along_y = modes(FULL)[(gy * 32 + by * 4 + dy).reshape(-1)]
    along_z_high, along_z_low = halves(modes(G3)[:, :ZC])
    kx = np.repeat(np.arange(FULL).reshape(N_GX, 16), 8, axis=1)
    place = np.arange(128)
    angle = (kx[:, None, :] * 4 * place[None, :, None] % FULL) * (2.0 * math.pi / FULL)
    phases = halves(np.concatenate([np.cos(angle), np.sin(angle)], axis=2)).transpose(1, 0, 2, 3)
    dx = np.arange(4)
    angle = kx[:, None, :] * dx[None, :, None] * (2.0 * math.pi / FULL)
    planes = np.concatenate([np.cos(angle) + np.sin(angle), np.cos(angle) - np.sin(angle)], axis=1)
    squares = 4.0 * np.sin(np.arange(FULL) * (math.pi / FULL)) ** 2
    deep = 4.0 * np.sin(np.arange(G3) * (math.pi / G3)) ** 2 + SCREENING
    return (
        halves(along_y),
        np.concatenate([along_z_high, along_z_high], axis=1),
        along_z_low,
        np.concatenate([along_z_high.T, along_z_low.T], axis=0),
        phases,
        planes.astype(np.float32),
        np.broadcast_to(squares[:, None, None], (FULL, 1, BP)).astype(np.float32),
        squares[None, :].astype(np.float32),
        np.broadcast_to(deep[:, None], (G3, BP)).astype(np.float32),
    )


def halves(value):
    high = value.astype(BF16)
    return high, (value - high.astype(F32)).astype(BF16)


def dot(left, right, dims):
    return lax.dot_general(left, right, dims, preferred_element_type=F32)


def lanes(shape):
    return lax.broadcasted_iota(jnp.int32, shape, 1)


def rows(shape):
    return lax.broadcasted_iota(jnp.int32, shape, 0)


def lane_sums(leaf, first, count):
    if count == 1:
        return leaf(first)
    half = count // 2
    left = lane_sums(leaf, first, half)
    right = lane_sums(leaf, first + half, half)
    upper = (lanes(left.shape) & half) != 0
    return jnp.where(upper, right, left) + pltpu.roll(
        jnp.where(upper, left, right), 128 - half, 1
    )


def swap_blocks(parts):
    parts = list(parts)
    block = lanes(parts[0].shape) // 8
    for bit in (8, 4, 2, 1):
        upper = (block & bit) != 0
        for i in range(16):
            if i & bit:
                continue
            a, b = parts[i], parts[i | bit]
            parts[i] = jnp.where(upper, pltpu.roll(b, 8 * bit, 1), a)
            parts[i | bit] = jnp.where(upper, b, pltpu.roll(a, 128 - 8 * bit, 1))
    return parts


def far_first(step, half):
    return half + (1 - 2 * (step % 2)) * ((step + 1) // 2)


def remote(source, target, axis, other, send_sem, recv_sem):
    pltpu.make_async_remote_copy(
        src_ref=source,
        dst_ref=target,
        send_sem=send_sem,
        recv_sem=recv_sem,
        device_id={axis: other},
        device_id_type=MESH,
    ).start()


def loop(count, step):
    def one(i, carry):
        step(i)
        return carry

    lax.fori_loop(0, count, one, 0)


def away(me, j, i, sign):
    x = lax.rem(me // N_Z + sign * X_OFFSETS[i] + N_X, N_X)
    z = lax.rem(me % N_Z + sign * Z_OFFSETS[j] + N_Z, N_Z)
    return x * N_Z + z


def send_columns(me, source, target, send_sem, recv_sem):
    def step(i):
        other = lax.rem(me + far_first(i, 8), N_GY)
        remote(source.at[other], target.at[me], "gy", other, send_sem, recv_sem)

    loop(N_GY - 1, step)


def wait_for(part, sem):
    pltpu.make_async_copy(part, part, sem).wait()


def body(
    charges_hbm,
    regions_hbm,
    inv_hbm,
    owner_hbm,
    index_hbm,
    target_hbm,
    source_hbm,
    projection_hbm,
    tiles_hbm,
    hy_hbm,
    hz_hbm,
    hz_low_hbm,
    hzt_hbm,
    phases_hbm,
    planes_hbm,
    along_x_hbm,
    along_y_hbm,
    along_z_hbm,
    out_ref,
    charges_ref,
    regions_ref,
    inv_ref,
    owner_ref,
    index_ref,
    target_ref,
    source_ref,
    projection_ref,
    tiles_ref,
    hy_ref,
    hz_ref,
    hz_low_ref,
    hzt_ref,
    phases_ref,
    planes_ref,
    along_x_ref,
    along_y_ref,
    along_z_ref,
    rows_ref,
    near_ref,
    kernel_ref,
    turn_ref,
    cells_ref,
    cells_t_ref,
    spread_ref,
    spread_high_ref,
    spread_low_ref,
    gather_ref,
    grid_ref,
    send_i,
    recv_i,
    send_b,
    recv_b,
    send_g,
    recv_g,
    send_f,
    recv_f,
    send_q,
    recv_q,
    send_r,
    recv_r,
    local_sem,
    send_sem,
    recv_sem,
    ring_sem,
    line_sem,
    back_sem,
):
    gx = lax.axis_index("gx")
    gy = lax.axis_index("gy")
    barrier = pltpu.get_barrier_semaphore()

    def greet(axis, other):
        pl.semaphore_signal(barrier, inc=1, device_id={axis: other}, device_id_type=MESH)

    last = N_GX - 1
    ring = N_Z - 1
    line = N_X - 1
    for j in range(ring):
        greet("gx", away(gx, j, line, 1))
    for i in range(line):
        greet("gx", away(gx, ring, i, 1))
    loop(N_GY - 1, lambda i: greet("gy", lax.rem(gy + far_first(i, 8), N_GY)))

    sources = [
        owner_hbm,
        index_hbm,
        inv_hbm,
        regions_hbm,
        charges_hbm,
        projection_hbm,
        target_hbm,
        source_hbm,
        tiles_hbm,
        phases_hbm.at[gx],
        planes_hbm.at[gx],
        along_x_hbm.at[gx * 16 + gy],
        along_y_hbm,
        along_z_hbm,
        hy_hbm,
        hz_hbm,
        hz_low_hbm,
        hzt_hbm,
    ]
    places = [
        owner_ref,
        index_ref,
        inv_ref,
        regions_ref,
        charges_ref,
        projection_ref,
        target_ref,
        source_ref,
        tiles_ref,
        phases_ref,
        planes_ref,
        along_x_ref,
        along_y_ref,
        along_z_ref,
        hy_ref,
        hz_ref,
        hz_low_ref,
        hzt_ref,
    ]
    loads = [
        pltpu.make_async_copy(source, place, local_sem.at[i])
        for i, (source, place) in enumerate(zip(sources, places))
    ]
    for load in loads:
        load.start()

    for load in loads[0:2]:
        load.wait()
    brick = index_ref[...]
    place = (owner_ref[...] * 4 + (brick >> 7)) * 128 + (brick & 15) * 8 + ((brick >> 4) & 7)
    place = jnp.concatenate([jnp.zeros((1, BP - NC), F32), place.astype(F32)], axis=1)
    send_i[...] = place

    for load in loads[2:6]:
        load.wait()
    regions = regions_ref[...]
    factor = jnp.zeros(regions.shape, F32)
    for k in range(NREG):
        factor = jnp.where(regions == k, inv_ref[0:1, k : k + 1], factor)
    scaled = charges_ref[...] * factor
    rows_ref[pl.ds(0, 16, stride=2), :] = scaled
    rows_ref[pl.ds(1, 16, stride=2), :] = pltpu.roll(scaled, CP, 1)
    charge_rows = rows_ref[...]
    bricks = charge_rows[:, 0:1] * projection_ref[:, 0:BP]
    for p in range(1, CP):
        bricks = bricks + charge_rows[:, p : p + 1] * projection_ref[:, p * BP : (p + 1) * BP]
    send_b[...] = bricks

    pl.semaphore_wait(barrier, ring + line + N_GY - 1)

    def to_ring(j):
        other = away(gx, j, line, 1)
        slot = j * N_X + line
        remote(send_i, recv_i.at[slot], "gx", other, send_sem.at[0], ring_sem.at[0, j])
        remote(send_b, recv_b.at[slot], "gx", other, send_sem.at[1], ring_sem.at[1, j])

    def to_line(index, block, j):
        for i in range(line):
            other = away(gx, ring, i, 1)
            slot = j * N_X + i
            remote(index, recv_i.at[slot], "gx", other, send_sem.at[2], line_sem.at[0, j // 2])
            remote(block, recv_b.at[slot], "gx", other, send_sem.at[3], line_sem.at[1, j // 2])

    for j in range(ring):
        to_ring(j)
    to_line(send_i, send_b, ring)
    recv_i[last] = place
    recv_b[last] = bricks

    for load in loads[6:9]:
        load.wait()
    shape = (NC, NC)
    eye = rows(shape) == lanes(shape)
    source_col = jnp.sum(
        jnp.where(eye, source_ref[...].astype(F32), 0.0), axis=1, keepdims=True
    )
    from_source = jnp.where(source_col == lanes(shape).astype(F32), 1.0, 0.0)
    near_charges = lax.dot_general(
        from_source, charge_rows, NN, precision=HIGHEST, preferred_element_type=F32
    )
    lower = lanes((NC, BP)) < CP
    near_charges = jnp.where(lower, near_charges, pltpu.roll(near_charges, CP, 1))

    def near_part(p):
        part = tiles_ref[:, p // 2 * BP : (p // 2 + 1) * BP] * near_charges
        return jnp.where(lower if p % 2 == 0 else jnp.logical_not(lower), part, 0.0)

    contrib = lane_sums(near_part, 0, CP)
    contrib = contrib + pltpu.roll(contrib, CP, 1)
    to_target = jnp.where(rows(shape) == target_ref[...], 1.0, 0.0)
    near_ref[...] = lax.dot_general(
        to_target, contrib, NN, precision=HIGHEST, preferred_element_type=F32
    )

    for load in loads[9:14]:
        load.wait()
    point, lane = rows((NC, BP)), lanes((NC, BP))
    for dx in range(4):
        for d in range(4):
            keep = (point // 8 == d) & (point % 8 == lane % 8)
            for part in range(2):
                wave = planes_ref[part * 4 + dx : part * 4 + dx + 1, :]
                c = (d * 2 + part) * BP
                spread_ref[dx * NC : (dx + 1) * NC, c : c + BP] = jnp.where(keep, wave, 0.0)
    high, low = halves(spread_ref[...])
    spread_high_ref[0:BP, :] = high
    spread_high_ref[BP : 2 * BP, :] = high
    spread_low_ref[...] = low
    for c in range(8):
        part = slice(c * BP, (c + 1) * BP)
        gather_ref[part, :] = jnp.concatenate(halves(spread_ref[:, part].T), axis=1)

    for c in range(4):
        part = slice(c * 128, (c + 1) * 128)
        kernel_ref[:, part] = (1.0 / (FULL * FULL * G3)) / (
            along_x_ref[...] + along_y_ref[:, part] + along_z_ref[...]
        )

    for j in reversed(range(ring)):
        slot = j * N_X + line
        wait_for(recv_i.at[slot], ring_sem.at[0, j])
        wait_for(recv_b.at[slot], ring_sem.at[1, j])
        to_line(recv_i.at[slot], recv_b.at[slot], j)

    tile = rows((128, 128))
    for g in range(GROUPS - 1, -1, -1):
        wait_for(recv_i.at[0 : 2 * line], line_sem.at[0, g])
        for j in (2 * g, 2 * g + 1):
            where = recv_i[N_X * j + line]
            for i in range(line):
                where = where + pltpu.roll(recv_i[N_X * j + i], NC * (i + 1), 1)
            where = where.astype(jnp.int32)
            at_cell = jnp.where((where & 127) == tile, 1.0, 0.0)
            at_cell_t = at_cell.T.astype(BF16)
            at_plane = jnp.where((where >> 7) == tile, 1.0, 0.0).T.astype(BF16)
            part = slice(j * 128, (j + 1) * 128)
            cells_ref[:, part] = at_cell.astype(BF16)
            cells_t_ref[part, :] = jnp.concatenate([at_cell_t, at_cell_t], axis=1)
            turn_ref[part, :] = dot(at_plane, phases_ref[0], NN) + dot(at_plane, phases_ref[1], NN)
        part = slice(g * SLOTS, (g + 1) * SLOTS)
        wait_for(recv_b.at[0 : 2 * line], line_sem.at[1, g])
        values = halves(recv_b[g * PER_GROUP : (g + 1) * PER_GROUP].reshape(SLOTS, BP))
        both = jnp.concatenate(values, axis=1)
        cosine, sine = turn_ref[part, 0:BP], turn_ref[part, BP : 2 * BP]
        cells = cells_ref[:, part]
        parts = dot(both, spread_high_ref[...], NN) + dot(values[0], spread_low_ref[...], NN)
        placed = []
        for d in range(4):
            c = d * 2 * BP
            placed.append(cosine * parts[:, c : c + BP] + sine * parts[:, c + BP : c + 2 * BP])
        placed = halves(jnp.concatenate(placed, axis=1))
        term = dot(cells, placed[0], NN) + dot(cells, placed[1], NN)
        grid_ref[...] = term if g == GROUPS - 1 else grid_ref[...] + term
    for d in range(4):
        lines = swap_blocks(
            [grid_ref[b * 8 : (b + 1) * 8, d * BP : (d + 1) * BP] for b in range(16)]
        )
        for k in range(16):
            send_g[k, d * 8 : (d + 1) * 8, :] = lines[k]
    send_columns(gy, send_g, recv_g, send_sem.at[4], recv_sem.at[0])
    recv_g[gy] = send_g[gy]

    for load in loads[14:18]:
        load.wait()
    wait_for(recv_g.at[0 : N_GY - 1], recv_sem.at[0])
    turned = recv_g[...].reshape(FULL, ZC).T
    high, low = halves(turned)
    field = dot(jnp.concatenate([high, low], axis=0), hy_ref[0], NN)
    field = field[0:ZC] + field[ZC : 2 * ZC] + dot(high, hy_ref[1], NN)
    high, low = halves(field)
    field = dot(hz_ref[...], jnp.concatenate([high, low], axis=0), NN) + dot(hz_low_ref[...], high, NN)
    high, low = halves(field * kernel_ref[...])
    field = dot(hzt_ref[...], high, NN)
    field = field[0:ZC] + field[ZC : 2 * ZC] + dot(hzt_ref[0:ZC, :], low, NN)
    high, low = halves(field)
    both = jnp.concatenate([high, low], axis=0)
    half = N_GY // 2
    for first in (0, half):
        others = [lax.rem(gy + far_first(i, half), N_GY) for i in range(first, first + half)]
        lines = [pl.ds(pl.multiple_of(other * 32, 32), 32) for other in others]
        field = dot(jnp.concatenate([hy_ref[0, part, :] for part in lines], axis=0), both, NT)
        field = (
            field[:, 0:ZC]
            + field[:, ZC : 2 * ZC]
            + dot(jnp.concatenate([hy_ref[1, part, :] for part in lines], axis=0), high, NT)
        )
        for i, other in enumerate(others):
            block = field[i * 32 : (i + 1) * 32, :]
            if first + i < N_GY - 1:
                send_f[first + i] = block
                remote(send_f.at[first + i], recv_f.at[gy], "gy", other, send_sem.at[5], recv_sem.at[1])
            else:
                recv_f[gy] = block
    wait_for(recv_f.at[0 : N_GY - 1], recv_sem.at[1])

    for d in range(4):
        parts = swap_blocks([recv_f[k, d * 8 : (d + 1) * 8, :] for k in range(16)])
        for b in range(16):
            grid_ref[b * 8 : (b + 1) * 8, d * BP : (d + 1) * BP] = parts[b]
    field = jnp.concatenate(halves(grid_ref[...]), axis=0)
    for g in range(GROUPS):
        part = slice(g * SLOTS, (g + 1) * SLOTS)
        lines = dot(cells_t_ref[part, :], field, NN)
        cosine, sine = turn_ref[part, 0:BP], turn_ref[part, BP : 2 * BP]
        turned = []
        for d in range(4):
            turned += [cosine * lines[:, d * BP : (d + 1) * BP], sine * lines[:, d * BP : (d + 1) * BP]]
        lines = halves(jnp.concatenate(turned, axis=1))
        total = dot(lines[0], gather_ref[...], NN)
        total = total[:, 0:BP] + total[:, BP : 2 * BP] + dot(lines[1], gather_ref[:, 0:BP], NN)
        send_q[g * PER_GROUP : (g + 1) * PER_GROUP] = total.reshape(PER_GROUP, NC, BP)

        for j in (2 * g, 2 * g + 1):
            slot = j * N_X
            for i in range(line):
                other = away(gx, ring, i, -1)
                remote(
                    send_q.at[slot + i], recv_q.at[j, i], "gx", other, send_sem.at[6], back_sem.at[j]
                )

    def add_line(j):
        wait_for(recv_q.at[j], back_sem.at[j])
        return send_q[j * N_X + line] + recv_q[j, 0] + recv_q[j, 1] + recv_q[j, 2]

    for j in range(ring):
        send_r[j] = add_line(j)
        other = away(gx, j, line, -1)
        remote(send_r.at[j], recv_r.at[j], "gx", other, send_sem.at[7], recv_sem.at[2])
    samples = add_line(ring)
    wait_for(recv_r, recv_sem.at[2])
    for j in range(ring):
        samples = samples + recv_r[j]

    def far_part(p):
        return projection_ref[:, p * BP : (p + 1) * BP] * samples

    far_field = lane_sums(far_part, 0, CP)
    far_field = far_field + pltpu.roll(far_field, CP, 1)
    rows_ref[...] = far_field + near_ref[...]
    even = rows_ref[pl.ds(0, 16, stride=2), :]
    odd = rows_ref[pl.ds(1, 16, stride=2), :]
    out_ref[...] = jnp.where(lanes((16, BP)) < CP, even, pltpu.roll(odd, CP, 1))

    wait_for(recv_i.at[0:ring], send_sem.at[0])
    wait_for(recv_b.at[0:ring], send_sem.at[1])
    wait_for(recv_i.at[0 : N_Z * line], send_sem.at[2])
    wait_for(recv_b.at[0 : N_Z * line], send_sem.at[3])
    wait_for(send_g.at[0 : N_GY - 1], send_sem.at[4])
    wait_for(send_f.at[0 : N_GY - 1], send_sem.at[5])
    wait_for(send_q.at[0 : N_Z * line], send_sem.at[6])
    wait_for(send_r.at[0:ring], send_sem.at[7])


def on_device(
    charges,
    regions,
    inv_permittivity,
    projection,
    slab_owner,
    brick_index,
    near_tiles,
    near_target,
    near_source,
):
    tables = [jnp.asarray(t) for t in host_tables()]
    in_hbm = pl.BlockSpec(memory_space=pltpu.HBM)
    small = pltpu.VMEM((1, NC), jnp.int32)
    bricks = pltpu.VMEM((N_GX, NC, BP), F32)
    columns = pltpu.VMEM((N_GY, 32, ZC), F32)
    out = pl.pallas_call(
        body,
        out_shape=jax.ShapeDtypeStruct((16, BP), F32),
        in_specs=[in_hbm] * 18,
        out_specs=pl.BlockSpec(memory_space=pltpu.VMEM),
        scratch_shapes=[
            pltpu.VMEM((16, BP), F32),
            pltpu.VMEM((16, BP), jnp.int32),
            pltpu.VMEM((1, NREG), F32),
            small,
            small,
            small,
            small,
            pltpu.VMEM((NC, CP * BP), F32),
            pltpu.VMEM((NC, CP * CP), F32),
            pltpu.VMEM((2, FULL, FULL), BF16),
            pltpu.VMEM((G3, 2 * ZC), BF16),
            pltpu.VMEM((G3, ZC), BF16),
            pltpu.VMEM((2 * ZC, G3), BF16),
            pltpu.VMEM((2, 128, 2 * BP), BF16),
            pltpu.VMEM((8, BP), F32),
            pltpu.VMEM((1, BP), F32),
            pltpu.VMEM((1, FULL), F32),
            pltpu.VMEM((G3, BP), F32),
            pltpu.VMEM((NC, BP), F32),
            pltpu.VMEM((NC, BP), F32),
            pltpu.VMEM((G3, FULL), F32),
            pltpu.VMEM((N_GX * NC, 2 * BP), F32),
            pltpu.VMEM((128, N_GX * NC), BF16),
            pltpu.VMEM((N_GX * NC, 2 * 128), BF16),
            pltpu.VMEM((BP, 2 * FULL), F32),
            pltpu.VMEM((2 * BP, 2 * FULL), BF16),
            pltpu.VMEM((BP, 2 * FULL), BF16),
            pltpu.VMEM((2 * FULL, 2 * BP), BF16),
            pltpu.VMEM((128, FULL), F32),
            pltpu.VMEM((1, BP), F32),
            pltpu.VMEM((N_GX, 1, BP), F32),
            pltpu.VMEM((NC, BP), F32),
            bricks,
            columns,
            columns,
            columns,
            columns,
            bricks,
            pltpu.VMEM((N_Z, N_X - 1, NC, BP), F32),
            pltpu.VMEM((N_Z - 1, NC, BP), F32),
            pltpu.VMEM((N_Z - 1, NC, BP), F32),
            pltpu.SemaphoreType.DMA((18,)),
            pltpu.SemaphoreType.DMA((8,)),
            pltpu.SemaphoreType.DMA((3,)),
            pltpu.SemaphoreType.DMA((2, N_Z - 1)),
            pltpu.SemaphoreType.DMA((2, GROUPS)),
            pltpu.SemaphoreType.DMA((N_Z,)),
        ],
        compiler_params=pltpu.CompilerParams(
            collective_id=0, has_side_effects=True, vmem_limit_bytes=60 * 1024 * 1024
        ),
    )(
        charges.reshape(16, BP),
        regions.reshape(16, BP),
        inv_permittivity.reshape(1, NREG),
        slab_owner.reshape(1, NC),
        brick_index.reshape(1, NC),
        near_target.reshape(1, NC),
        near_source.reshape(1, NC),
        projection,
        near_tiles,
        *tables,
    )
    return out.reshape(-1)


def solution(mesh):
    both = P(("gx", "gy"))
    wide = P(("gx", "gy"), None)
    return jax.shard_map(
        on_device,
        mesh=mesh,
        in_specs=(both, both, P(), wide, both, both, wide, both, both),
        out_specs=both,
        check_vma=False,
    )
```

```python
import functools
import math

import jax
import jax.numpy as jnp
import numpy as np
from jax import lax
from jax.experimental import pallas as pl
from jax.experimental.pallas import tpu as pltpu
from jax.sharding import PartitionSpec as P

CP = 64
NREG = 8
N_GX = 32
N_GY = 16
N_X = 4
N_Z = 8
NC = 32
BP = 128
FULL = 512
G3 = 256
ZC = 128
SCREENING = 0.001
Z_OFFSETS = (4, 3, 5, 2, 6, 1, 7, 0)
X_OFFSETS = (2, 1, 3, 0)
NEAR = (5, 6)
GROUPS = 4
PER_GROUP = N_GX // GROUPS
SLOTS = PER_GROUP * NC

F32 = jnp.float32
BF16 = jnp.bfloat16
HIGHEST = lax.Precision.HIGHEST
MESH = pl.DeviceIdType.MESH

NN = (((1,), (0,)), ((), ()))
NT = (((1,), (1,)), ((), ()))


@functools.lru_cache(maxsize=None)
def host_tables():
    def halves(table):
        table = table.astype(np.float32)
        high = table.astype(BF16)
        low = (table - high.astype(np.float32)).astype(BF16)
        return np.stack([high, low])

    def modes(length):
        n = np.arange(length)
        angle = (n[:, None] * n[None, :] % length) * (2.0 * math.pi / length)
        return np.cos(angle) + np.sin(angle)

    gy, dy, by = np.meshgrid(np.arange(N_GY), np.arange(4), np.arange(8), indexing="ij")
    along_y = modes(FULL)[(gy * 32 + by * 4 + dy).reshape(-1)]
    along_z_high, along_z_low = halves(modes(G3)[:, :ZC])
    kx = np.repeat(np.arange(FULL).reshape(N_GX, 16), 8, axis=1)
    place = np.arange(128)
    angle = (kx[:, None, :] * 4 * place[None, :, None] % FULL) * (2.0 * math.pi / FULL)
    phases = halves(np.concatenate([np.cos(angle), np.sin(angle)], axis=2)).transpose(1, 0, 2, 3)
    dx = np.arange(4)
    angle = kx[:, None, :] * dx[None, :, None] * (2.0 * math.pi / FULL)
    planes = np.concatenate([np.cos(angle) + np.sin(angle), np.cos(angle) - np.sin(angle)], axis=1)
    squares = 4.0 * np.sin(np.arange(FULL) * (math.pi / FULL)) ** 2
    deep = 4.0 * np.sin(np.arange(G3) * (math.pi / G3)) ** 2 + SCREENING
    return (
        halves(along_y),
        np.concatenate([along_z_high, along_z_high], axis=1),
        along_z_low,
        np.concatenate([along_z_high.T, along_z_low.T], axis=0),
        phases,
        planes.astype(np.float32),
        np.broadcast_to(squares[:, None, None], (FULL, 1, BP)).astype(np.float32),
        squares[None, :].astype(np.float32),
        np.broadcast_to(deep[:, None], (G3, BP)).astype(np.float32),
    )


def halves(value):
    high = value.astype(BF16)
    return high, (value - high.astype(F32)).astype(BF16)


def dot(left, right, dims):
    return lax.dot_general(left, right, dims, preferred_element_type=F32)


def lanes(shape):
    return lax.broadcasted_iota(jnp.int32, shape, 1)


def rows(shape):
    return lax.broadcasted_iota(jnp.int32, shape, 0)


def lane_sums(leaf, first, count):
    if count == 1:
        return leaf(first)
    half = count // 2
    left = lane_sums(leaf, first, half)
    right = lane_sums(leaf, first + half, half)
    upper = (lanes(left.shape) & half) != 0
    return jnp.where(upper, right, left) + pltpu.roll(
        jnp.where(upper, left, right), 128 - half, 1
    )


def swap_blocks(parts):
    parts = list(parts)
    block = lanes(parts[0].shape) // 8
    for bit in (8, 4, 2, 1):
        upper = (block & bit) != 0
        for i in range(16):
            if i & bit:
                continue
            a, b = parts[i], parts[i | bit]
            parts[i] = jnp.where(upper, pltpu.roll(b, 8 * bit, 1), a)
            parts[i | bit] = jnp.where(upper, b, pltpu.roll(a, 128 - 8 * bit, 1))
    return parts


def far_first(step, half):
    return half + (1 - 2 * (step % 2)) * ((step + 1) // 2)


def remote(source, target, axis, other, send_sem, recv_sem):
    pltpu.make_async_remote_copy(
        src_ref=source,
        dst_ref=target,
        send_sem=send_sem,
        recv_sem=recv_sem,
        device_id={axis: other},
        device_id_type=MESH,
    ).start()


def loop(count, step):
    def one(i, carry):
        step(i)
        return carry

    lax.fori_loop(0, count, one, 0)


def away(me, j, i, sign):
    x = lax.rem(me // N_Z + sign * X_OFFSETS[i] + N_X, N_X)
    z = lax.rem(me % N_Z + sign * Z_OFFSETS[j] + N_Z, N_Z)
    return x * N_Z + z


def send_columns(me, source, target, send_sem, recv_sem):
    def step(i):
        other = lax.rem(me + far_first(i, 8), N_GY)
        remote(source.at[other], target.at[me], "gy", other, send_sem, recv_sem)

    loop(N_GY - 1, step)


def wait_for(part, sem):
    pltpu.make_async_copy(part, part, sem).wait()


def body(
    charges_hbm,
    regions_hbm,
    inv_hbm,
    owner_hbm,
    index_hbm,
    target_hbm,
    source_hbm,
    projection_hbm,
    tiles_hbm,
    hy_hbm,
    hz_hbm,
    hz_low_hbm,
    hzt_hbm,
    phases_hbm,
    planes_hbm,
    along_x_hbm,
    along_y_hbm,
    along_z_hbm,
    out_ref,
    charges_ref,
    regions_ref,
    inv_ref,
    owner_ref,
    index_ref,
    target_ref,
    source_ref,
    projection_ref,
    tiles_ref,
    hy_ref,
    hz_ref,
    hz_low_ref,
    hzt_ref,
    phases_ref,
    planes_ref,
    along_x_ref,
    along_y_ref,
    along_z_ref,
    rows_ref,
    near_ref,
    kernel_ref,
    turn_ref,
    cells_ref,
    cells_t_ref,
    spread_ref,
    spread_high_ref,
    spread_low_ref,
    gather_ref,
    grid_ref,
    send_i,
    recv_i,
    send_b,
    recv_b,
    send_g,
    recv_g,
    send_f,
    recv_f,
    send_q,
    recv_q,
    send_r,
    recv_r,
    recv_n,
    local_sem,
    send_sem,
    recv_sem,
    ring_sem,
    line_sem,
    own_sem,
    back_sem,
    near_sem,
):
    gx = lax.axis_index("gx")
    gy = lax.axis_index("gy")
    barrier = pltpu.get_barrier_semaphore()

    def greet(axis, other):
        pl.semaphore_signal(barrier, inc=1, device_id={axis: other}, device_id_type=MESH)

    last = N_GX - 1
    ring = N_Z - 1
    line = N_X - 1
    for j in range(ring):
        greet("gx", away(gx, j, line, 1))
    for i in range(line):
        greet("gx", away(gx, ring, i, 1))
    loop(N_GY - 1, lambda i: greet("gy", lax.rem(gy + far_first(i, 8), N_GY)))

    sources = [
        owner_hbm,
        index_hbm,
        inv_hbm,
        regions_hbm,
        charges_hbm,
        projection_hbm,
        target_hbm,
        source_hbm,
        tiles_hbm,
        phases_hbm.at[gx],
        planes_hbm.at[gx],
        along_x_hbm.at[gx * 16 + gy],
        along_y_hbm,
        along_z_hbm,
        hy_hbm,
        hz_hbm,
        hz_low_hbm,
        hzt_hbm,
    ]
    places = [
        owner_ref,
        index_ref,
        inv_ref,
        regions_ref,
        charges_ref,
        projection_ref,
        target_ref,
        source_ref,
        tiles_ref,
        phases_ref,
        planes_ref,
        along_x_ref,
        along_y_ref,
        along_z_ref,
        hy_ref,
        hz_ref,
        hz_low_ref,
        hzt_ref,
    ]
    loads = [
        pltpu.make_async_copy(source, place, local_sem.at[i])
        for i, (source, place) in enumerate(zip(sources, places))
    ]
    for load in loads:
        load.start()

    for load in loads[0:2]:
        load.wait()
    brick = index_ref[...]
    place = (owner_ref[...] * 4 + (brick >> 7)) * 128 + (brick & 15) * 8 + ((brick >> 4) & 7)
    place = jnp.concatenate([jnp.zeros((1, BP - NC), F32), place.astype(F32)], axis=1)
    send_i[...] = place

    for load in loads[2:6]:
        load.wait()
    regions = regions_ref[...]
    factor = jnp.zeros(regions.shape, F32)
    for k in range(NREG):
        factor = jnp.where(regions == k, inv_ref[0:1, k : k + 1], factor)
    scaled = charges_ref[...] * factor
    rows_ref[pl.ds(0, 16, stride=2), :] = scaled
    rows_ref[pl.ds(1, 16, stride=2), :] = pltpu.roll(scaled, CP, 1)
    charge_rows = rows_ref[...]
    bricks = charge_rows[:, 0:1] * projection_ref[:, 0:BP]
    for p in range(1, CP):
        bricks = bricks + charge_rows[:, p : p + 1] * projection_ref[:, p * BP : (p + 1) * BP]
    send_b[...] = bricks

    pl.semaphore_wait(barrier, ring + line + N_GY - 1)

    def to_ring(j):
        other = away(gx, j, line, 1)
        slot = j * N_X + line
        remote(send_i, recv_i.at[slot], "gx", other, send_sem.at[0], ring_sem.at[0, j])
        remote(send_b, recv_b.at[slot], "gx", other, send_sem.at[1], ring_sem.at[1, j])

    def to_line(index, block, j):
        for i in range(line):
            other = away(gx, ring, i, 1)
            slot = j * N_X + i
            remote(index, recv_i.at[slot], "gx", other, send_sem.at[2], line_sem.at[0, j // 2])
            remote(block, recv_b.at[slot], "gx", other, send_sem.at[3], line_sem.at[1, j // 2])

    for j in (5, 6, 3, 4, 1, 2, 0):
        to_ring(j)
    to_line(send_i, send_b, ring)
    recv_i[last] = place
    recv_b[last] = bricks

    for load in loads[6:9]:
        load.wait()
    shape = (NC, NC)
    eye = rows(shape) == lanes(shape)
    source_col = jnp.sum(
        jnp.where(eye, source_ref[...].astype(F32), 0.0), axis=1, keepdims=True
    )
    from_source = jnp.where(source_col == lanes(shape).astype(F32), 1.0, 0.0)
    near_charges = lax.dot_general(
        from_source, charge_rows, NN, precision=HIGHEST, preferred_element_type=F32
    )
    lower = lanes((NC, BP)) < CP
    near_charges = jnp.where(lower, near_charges, pltpu.roll(near_charges, CP, 1))

    def near_part(p):
        part = tiles_ref[:, p // 2 * BP : (p // 2 + 1) * BP] * near_charges
        return jnp.where(lower if p % 2 == 0 else jnp.logical_not(lower), part, 0.0)

    contrib = lane_sums(near_part, 0, CP)
    contrib = contrib + pltpu.roll(contrib, CP, 1)
    to_target = jnp.where(rows(shape) == target_ref[...], 1.0, 0.0)
    near_ref[...] = lax.dot_general(
        to_target, contrib, NN, precision=HIGHEST, preferred_element_type=F32
    )

    for load in loads[9:14]:
        load.wait()
    point, lane = rows((NC, BP)), lanes((NC, BP))
    for dx in range(4):
        for d in range(4):
            keep = (point // 8 == d) & (point % 8 == lane % 8)
            for part in range(2):
                wave = planes_ref[part * 4 + dx : part * 4 + dx + 1, :]
                c = (d * 2 + part) * BP
                spread_ref[dx * NC : (dx + 1) * NC, c : c + BP] = jnp.where(keep, wave, 0.0)
    high, low = halves(spread_ref[...])
    spread_high_ref[0:BP, :] = high
    spread_high_ref[BP : 2 * BP, :] = high
    spread_low_ref[...] = low
    for c in range(8):
        part = slice(c * BP, (c + 1) * BP)
        gather_ref[part, :] = jnp.concatenate(halves(spread_ref[:, part].T), axis=1)

    for c in range(4):
        part = slice(c * 128, (c + 1) * 128)
        kernel_ref[:, part] = (1.0 / (FULL * FULL * G3)) / (
            along_x_ref[...] + along_y_ref[:, part] + along_z_ref[...]
        )

    for j in (5, 6, 3, 4, 1, 2, 0):
        slot = j * N_X + line
        wait_for(recv_i.at[slot], ring_sem.at[0, j])
        wait_for(recv_b.at[slot], ring_sem.at[1, j])
        to_line(recv_i.at[slot], recv_b.at[slot], j)

    tile = rows((128, 128))
    for g in range(GROUPS - 1, -1, -1):
        wait_for(recv_i.at[0 : 2 * line], line_sem.at[0, g])
        for j in (2 * g, 2 * g + 1):
            where = recv_i[N_X * j + line]
            for i in range(line):
                where = where + pltpu.roll(recv_i[N_X * j + i], NC * (i + 1), 1)
            where = where.astype(jnp.int32)
            at_cell = jnp.where((where & 127) == tile, 1.0, 0.0)
            at_cell_t = at_cell.T.astype(BF16)
            at_plane = jnp.where((where >> 7) == tile, 1.0, 0.0).T.astype(BF16)
            part = slice(j * 128, (j + 1) * 128)
            cells_ref[:, part] = at_cell.astype(BF16)
            cells_t_ref[part, :] = jnp.concatenate([at_cell_t, at_cell_t], axis=1)
            turn_ref[part, :] = dot(at_plane, phases_ref[0], NN) + dot(at_plane, phases_ref[1], NN)
        part = slice(g * SLOTS, (g + 1) * SLOTS)
        wait_for(recv_b.at[0 : 2 * line], line_sem.at[1, g])
        values = halves(recv_b[g * PER_GROUP : (g + 1) * PER_GROUP].reshape(SLOTS, BP))
        both = jnp.concatenate(values, axis=1)
        cosine, sine = turn_ref[part, 0:BP], turn_ref[part, BP : 2 * BP]
        cells = cells_ref[:, part]
        parts = dot(both, spread_high_ref[...], NN) + dot(values[0], spread_low_ref[...], NN)
        placed = []
        for d in range(4):
            c = d * 2 * BP
            placed.append(cosine * parts[:, c : c + BP] + sine * parts[:, c + BP : c + 2 * BP])
        placed = halves(jnp.concatenate(placed, axis=1))
        term = dot(cells, placed[0], NN) + dot(cells, placed[1], NN)
        grid_ref[...] = term if g == GROUPS - 1 else grid_ref[...] + term
    for d in range(4):
        lines = swap_blocks(
            [grid_ref[b * 8 : (b + 1) * 8, d * BP : (d + 1) * BP] for b in range(16)]
        )
        for k in range(16):
            send_g[k, d * 8 : (d + 1) * 8, :] = lines[k]
    send_columns(gy, send_g, recv_g, send_sem.at[4], recv_sem.at[0])
    recv_g[gy] = send_g[gy]

    for load in loads[14:18]:
        load.wait()
    wait_for(recv_g.at[0 : N_GY - 1], recv_sem.at[0])
    turned = recv_g[...].reshape(FULL, ZC).T
    high, low = halves(turned)
    field = dot(jnp.concatenate([high, low], axis=0), hy_ref[0], NN)
    field = field[0:ZC] + field[ZC : 2 * ZC] + dot(high, hy_ref[1], NN)
    high, low = halves(field)
    field = dot(hz_ref[...], jnp.concatenate([high, low], axis=0), NN) + dot(hz_low_ref[...], high, NN)
    high, low = halves(field * kernel_ref[...])
    field = dot(hzt_ref[...], high, NN)
    field = field[0:ZC] + field[ZC : 2 * ZC] + dot(hzt_ref[0:ZC, :], low, NN)
    high, low = halves(field)
    both = jnp.concatenate([high, low], axis=0)
    half = N_GY // 2
    for first in (0, half):
        others = [lax.rem(gy + far_first(i, half), N_GY) for i in range(first, first + half)]
        lines = [pl.ds(pl.multiple_of(other * 32, 32), 32) for other in others]
        field = dot(jnp.concatenate([hy_ref[0, part, :] for part in lines], axis=0), both, NT)
        field = (
            field[:, 0:ZC]
            + field[:, ZC : 2 * ZC]
            + dot(jnp.concatenate([hy_ref[1, part, :] for part in lines], axis=0), high, NT)
        )
        for i, other in enumerate(others):
            block = field[i * 32 : (i + 1) * 32, :]
            if first + i < N_GY - 1:
                send_f[first + i] = block
                remote(send_f.at[first + i], recv_f.at[gy], "gy", other, send_sem.at[5], recv_sem.at[1])
            else:
                recv_f[gy] = block
    wait_for(recv_f.at[0 : N_GY - 1], recv_sem.at[1])

    for d in range(4):
        parts = swap_blocks([recv_f[k, d * 8 : (d + 1) * 8, :] for k in range(16)])
        for b in range(16):
            grid_ref[b * 8 : (b + 1) * 8, d * BP : (d + 1) * BP] = parts[b]
    field = jnp.concatenate(halves(grid_ref[...]), axis=0)

    def back_on_line(j):
        for i in range(line):
            other = away(gx, ring, i, -1)
            remote(
                send_q.at[j * N_X + i], recv_q.at[j, i], "gx", other, send_sem.at[6], back_sem.at[j]
            )

    for first, end in ((1, 3), (0, 1), (5, 7), (3, 5), (7, 8)):
        part = slice(first * BP, end * BP)
        lines = dot(cells_t_ref[part, :], field, NN)
        cosine, sine = turn_ref[part, 0:BP], turn_ref[part, BP : 2 * BP]
        turned = []
        for d in range(4):
            turned += [cosine * lines[:, d * BP : (d + 1) * BP], sine * lines[:, d * BP : (d + 1) * BP]]
        lines = halves(jnp.concatenate(turned, axis=1))
        total = dot(lines[0], gather_ref[...], NN)
        total = total[:, 0:BP] + total[:, BP : 2 * BP] + dot(lines[1], gather_ref[:, 0:BP], NN)
        send_q[first * N_X : end * N_X] = total.reshape((end - first) * N_X, NC, BP)
        for j in range(first, end):
            slot = j * N_X
            if j in NEAR:
                other = away(gx, j, line, -1)
                remote(
                    send_q.at[slot + line], recv_r.at[j], "gx", other, send_sem.at[7], recv_sem.at[2]
                )
                near = j - NEAR[0]
                for i in range(line):
                    remote(
                        send_q.at[slot + i],
                        recv_n.at[near, i],
                        "gx",
                        other,
                        send_sem.at[6],
                        near_sem.at[near],
                    )
            elif j < ring:
                back_on_line(j)

    for near in range(2):
        wait_for(recv_n.at[near], near_sem.at[near])
    for i in range(line):
        slot = ring * N_X + i
        send_q[slot] = send_q[slot] + recv_n[0, i] + recv_n[1, i]
    back_on_line(ring)

    def add_line(j):
        wait_for(recv_q.at[j], back_sem.at[j])
        return send_q[j * N_X + line] + recv_q[j, 0] + recv_q[j, 1] + recv_q[j, 2]

    for j in range(NEAR[0]):
        send_r[j] = add_line(j)
        other = away(gx, j, line, -1)
        remote(send_r.at[j], recv_r.at[j], "gx", other, send_sem.at[7], recv_sem.at[2])
    samples = add_line(ring)
    wait_for(recv_r, recv_sem.at[2])
    for j in range(ring):
        samples = samples + recv_r[j]

    def far_part(p):
        return projection_ref[:, p * BP : (p + 1) * BP] * samples

    far_field = lane_sums(far_part, 0, CP)
    far_field = far_field + pltpu.roll(far_field, CP, 1)
    rows_ref[...] = far_field + near_ref[...]
    even = rows_ref[pl.ds(0, 16, stride=2), :]
    odd = rows_ref[pl.ds(1, 16, stride=2), :]
    out_ref[...] = jnp.where(lanes((16, BP)) < CP, even, pltpu.roll(odd, CP, 1))

    wait_for(recv_i.at[0:ring], send_sem.at[0])
    wait_for(recv_b.at[0:ring], send_sem.at[1])
    wait_for(recv_i.at[0 : N_Z * line], send_sem.at[2])
    wait_for(recv_b.at[0 : N_Z * line], send_sem.at[3])
    wait_for(send_g.at[0 : N_GY - 1], send_sem.at[4])
    wait_for(send_f.at[0 : N_GY - 1], send_sem.at[5])
    wait_for(send_q.at[0 : N_Z * line], send_sem.at[6])
    wait_for(send_r.at[0:ring], send_sem.at[7])


def on_device(
    charges,
    regions,
    inv_permittivity,
    projection,
    slab_owner,
    brick_index,
    near_tiles,
    near_target,
    near_source,
):
    tables = [jnp.asarray(t) for t in host_tables()]
    in_hbm = pl.BlockSpec(memory_space=pltpu.HBM)
    small = pltpu.VMEM((1, NC), jnp.int32)
    bricks = pltpu.VMEM((N_GX, NC, BP), F32)
    columns = pltpu.VMEM((N_GY, 32, ZC), F32)
    out = pl.pallas_call(
        body,
        out_shape=jax.ShapeDtypeStruct((16, BP), F32),
        in_specs=[in_hbm] * 18,
        out_specs=pl.BlockSpec(memory_space=pltpu.VMEM),
        scratch_shapes=[
            pltpu.VMEM((16, BP), F32),
            pltpu.VMEM((16, BP), jnp.int32),
            pltpu.VMEM((1, NREG), F32),
            small,
            small,
            small,
            small,
            pltpu.VMEM((NC, CP * BP), F32),
            pltpu.VMEM((NC, CP * CP), F32),
            pltpu.VMEM((2, FULL, FULL), BF16),
            pltpu.VMEM((G3, 2 * ZC), BF16),
            pltpu.VMEM((G3, ZC), BF16),
            pltpu.VMEM((2 * ZC, G3), BF16),
            pltpu.VMEM((2, 128, 2 * BP), BF16),
            pltpu.VMEM((8, BP), F32),
            pltpu.VMEM((1, BP), F32),
            pltpu.VMEM((1, FULL), F32),
            pltpu.VMEM((G3, BP), F32),
            pltpu.VMEM((NC, BP), F32),
            pltpu.VMEM((NC, BP), F32),
            pltpu.VMEM((G3, FULL), F32),
            pltpu.VMEM((N_GX * NC, 2 * BP), F32),
            pltpu.VMEM((128, N_GX * NC), BF16),
            pltpu.VMEM((N_GX * NC, 2 * 128), BF16),
            pltpu.VMEM((BP, 2 * FULL), F32),
            pltpu.VMEM((2 * BP, 2 * FULL), BF16),
            pltpu.VMEM((BP, 2 * FULL), BF16),
            pltpu.VMEM((2 * FULL, 2 * BP), BF16),
            pltpu.VMEM((128, FULL), F32),
            pltpu.VMEM((1, BP), F32),
            pltpu.VMEM((N_GX, 1, BP), F32),
            pltpu.VMEM((NC, BP), F32),
            bricks,
            columns,
            columns,
            columns,
            columns,
            bricks,
            pltpu.VMEM((N_Z, N_X - 1, NC, BP), F32),
            pltpu.VMEM((N_Z - 1, NC, BP), F32),
            pltpu.VMEM((N_Z - 1, NC, BP), F32),
            pltpu.VMEM((2, N_X - 1, NC, BP), F32),
            pltpu.SemaphoreType.DMA((18,)),
            pltpu.SemaphoreType.DMA((8,)),
            pltpu.SemaphoreType.DMA((3,)),
            pltpu.SemaphoreType.DMA((2, N_Z - 1)),
            pltpu.SemaphoreType.DMA((2, N_Z - 1)),
            pltpu.SemaphoreType.DMA((2, N_X - 1)),
            pltpu.SemaphoreType.DMA((N_Z,)),
            pltpu.SemaphoreType.DMA((2,)),
        ],
        compiler_params=pltpu.CompilerParams(
            collective_id=0, has_side_effects=True, vmem_limit_bytes=60 * 1024 * 1024
        ),
    )(
        charges.reshape(16, BP),
        regions.reshape(16, BP),
        inv_permittivity.reshape(1, NREG),
        slab_owner.reshape(1, NC),
        brick_index.reshape(1, NC),
        near_target.reshape(1, NC),
        near_source.reshape(1, NC),
        projection,
        near_tiles,
        *tables,
    )
    return out.reshape(-1)


def solution(mesh):
    both = P(("gx", "gy"))
    wide = P(("gx", "gy"), None)
    return jax.shard_map(
        on_device,
        mesh=mesh,
        in_specs=(both, both, P(), wide, both, both, wide, both, both),
        out_specs=both,
        check_vma=False,
    )
```

```python
import functools
import math

import jax
import jax.numpy as jnp
import numpy as np
from jax import lax
from jax.experimental import pallas as pl
from jax.experimental.pallas import tpu as pltpu
from jax.sharding import PartitionSpec as P

CP = 64
NREG = 8
N_GX = 32
N_GY = 16
N_X = 4
N_Z = 8
NC = 32
BP = 128
FULL = 512
G3 = 256
ZC = 128
SCREENING = 0.001
Z_OFFSETS = (4, 3, 5, 2, 6, 1, 7, 0)
X_OFFSETS = (2, 1, 3, 0)
NEAR = (5, 6)
GROUPS = 4
PER_GROUP = N_GX // GROUPS
SLOTS = PER_GROUP * NC

F32 = jnp.float32
BF16 = jnp.bfloat16
HIGHEST = lax.Precision.HIGHEST
MESH = pl.DeviceIdType.MESH

NN = (((1,), (0,)), ((), ()))
NT = (((1,), (1,)), ((), ()))


@functools.lru_cache(maxsize=None)
def host_tables():
    def halves(table):
        table = table.astype(np.float32)
        high = table.astype(BF16)
        low = (table - high.astype(np.float32)).astype(BF16)
        return np.stack([high, low])

    def modes(length):
        n = np.arange(length)
        angle = (n[:, None] * n[None, :] % length) * (2.0 * math.pi / length)
        return np.cos(angle) + np.sin(angle)

    gy, dy, by = np.meshgrid(np.arange(N_GY), np.arange(4), np.arange(8), indexing="ij")
    along_y = modes(FULL)[(gy * 32 + by * 4 + dy).reshape(-1)]
    along_z_high, along_z_low = halves(modes(G3)[:, :ZC])
    kx = np.repeat(np.arange(FULL).reshape(N_GX, 16), 8, axis=1)
    place = np.arange(128)
    angle = (kx[:, None, :] * 4 * place[None, :, None] % FULL) * (2.0 * math.pi / FULL)
    phases = halves(np.concatenate([np.cos(angle), np.sin(angle)], axis=2)).transpose(1, 0, 2, 3)
    dx = np.arange(4)
    angle = kx[:, None, :] * dx[None, :, None] * (2.0 * math.pi / FULL)
    planes = np.concatenate([np.cos(angle) + np.sin(angle), np.cos(angle) - np.sin(angle)], axis=1)
    squares = 4.0 * np.sin(np.arange(FULL) * (math.pi / FULL)) ** 2
    deep = 4.0 * np.sin(np.arange(G3) * (math.pi / G3)) ** 2 + SCREENING
    return (
        halves(along_y),
        np.concatenate([along_z_high, along_z_high], axis=1),
        along_z_low,
        np.concatenate([along_z_high.T, along_z_low.T], axis=0),
        phases,
        planes.astype(np.float32),
        np.broadcast_to(squares[:, None, None], (FULL, 1, BP)).astype(np.float32),
        squares[None, :].astype(np.float32),
        np.broadcast_to(deep[:, None], (G3, BP)).astype(np.float32),
    )


def halves(value):
    high = value.astype(BF16)
    return high, (value - high.astype(F32)).astype(BF16)


def dot(left, right, dims):
    return lax.dot_general(left, right, dims, preferred_element_type=F32)


def lanes(shape):
    return lax.broadcasted_iota(jnp.int32, shape, 1)


def rows(shape):
    return lax.broadcasted_iota(jnp.int32, shape, 0)


def lane_sums(leaf, first, count):
    if count == 1:
        return leaf(first)
    half = count // 2
    left = lane_sums(leaf, first, half)
    right = lane_sums(leaf, first + half, half)
    upper = (lanes(left.shape) & half) != 0
    return jnp.where(upper, right, left) + pltpu.roll(
        jnp.where(upper, left, right), 128 - half, 1
    )


def swap_blocks(parts):
    parts = list(parts)
    block = lanes(parts[0].shape) // 8
    for bit in (8, 4, 2, 1):
        upper = (block & bit) != 0
        for i in range(16):
            if i & bit:
                continue
            a, b = parts[i], parts[i | bit]
            parts[i] = jnp.where(upper, pltpu.roll(b, 8 * bit, 1), a)
            parts[i | bit] = jnp.where(upper, b, pltpu.roll(a, 128 - 8 * bit, 1))
    return parts


def far_first(step, half):
    return half + (1 - 2 * (step % 2)) * ((step + 1) // 2)


def remote(source, target, axis, other, send_sem, recv_sem):
    pltpu.make_async_remote_copy(
        src_ref=source,
        dst_ref=target,
        send_sem=send_sem,
        recv_sem=recv_sem,
        device_id={axis: other},
        device_id_type=MESH,
    ).start()


def loop(count, step):
    def one(i, carry):
        step(i)
        return carry

    lax.fori_loop(0, count, one, 0)


def away(me, j, i, sign):
    x = lax.rem(me // N_Z + sign * X_OFFSETS[i] + N_X, N_X)
    z = lax.rem(me % N_Z + sign * Z_OFFSETS[j] + N_Z, N_Z)
    return x * N_Z + z


ORDER = (6, 10, 7, 9, 8, 5, 11, 4, 12, 3, 13, 2, 14, 1, 15, 0)


def send_columns(me, source, target, send_sem, recv_sem):
    for o in ORDER[:-1]:
        other = lax.rem(me + o, N_GY)
        remote(source.at[other], target.at[me], "gy", other, send_sem, recv_sem)


def wait_for(part, sem):
    pltpu.make_async_copy(part, part, sem).wait()


def body(
    charges_hbm,
    regions_hbm,
    inv_hbm,
    owner_hbm,
    index_hbm,
    target_hbm,
    source_hbm,
    projection_hbm,
    tiles_hbm,
    hy_hbm,
    hz_hbm,
    hz_low_hbm,
    hzt_hbm,
    phases_hbm,
    planes_hbm,
    along_x_hbm,
    along_y_hbm,
    along_z_hbm,
    out_ref,
    charges_ref,
    regions_ref,
    inv_ref,
    owner_ref,
    index_ref,
    target_ref,
    source_ref,
    projection_ref,
    tiles_ref,
    hy_ref,
    hz_ref,
    hz_low_ref,
    hzt_ref,
    phases_ref,
    planes_ref,
    along_x_ref,
    along_y_ref,
    along_z_ref,
    rows_ref,
    near_ref,
    kernel_ref,
    turn_ref,
    cells_ref,
    cells_t_ref,
    spread_ref,
    spread_high_ref,
    spread_low_ref,
    gather_ref,
    grid_ref,
    send_i,
    recv_i,
    send_b,
    recv_b,
    send_g,
    recv_g,
    send_f,
    recv_f,
    send_q,
    recv_q,
    send_r,
    recv_r,
    recv_n,
    local_sem,
    send_sem,
    recv_sem,
    ring_sem,
    line_sem,
    own_sem,
    back_sem,
    near_sem,
):
    gx = lax.axis_index("gx")
    gy = lax.axis_index("gy")
    barrier = pltpu.get_barrier_semaphore()

    def greet(axis, other):
        pl.semaphore_signal(barrier, inc=1, device_id={axis: other}, device_id_type=MESH)

    last = N_GX - 1
    ring = N_Z - 1
    line = N_X - 1
    for j in range(ring):
        greet("gx", away(gx, j, line, 1))
    for i in range(line):
        greet("gx", away(gx, ring, i, 1))
    loop(N_GY - 1, lambda i: greet("gy", lax.rem(gy + far_first(i, 8), N_GY)))

    sources = [
        owner_hbm,
        index_hbm,
        inv_hbm,
        regions_hbm,
        charges_hbm,
        projection_hbm,
        target_hbm,
        source_hbm,
        tiles_hbm,
        phases_hbm.at[gx],
        planes_hbm.at[gx],
        along_x_hbm.at[gx * 16 + gy],
        along_y_hbm,
        along_z_hbm,
        hy_hbm,
        hz_hbm,
        hz_low_hbm,
        hzt_hbm,
    ]
    places = [
        owner_ref,
        index_ref,
        inv_ref,
        regions_ref,
        charges_ref,
        projection_ref,
        target_ref,
        source_ref,
        tiles_ref,
        phases_ref,
        planes_ref,
        along_x_ref,
        along_y_ref,
        along_z_ref,
        hy_ref,
        hz_ref,
        hz_low_ref,
        hzt_ref,
    ]
    loads = [
        pltpu.make_async_copy(source, place, local_sem.at[i])
        for i, (source, place) in enumerate(zip(sources, places))
    ]
    for load in loads:
        load.start()

    for load in loads[0:2]:
        load.wait()
    brick = index_ref[...]
    place = (owner_ref[...] * 4 + (brick >> 7)) * 128 + (brick & 15) * 8 + ((brick >> 4) & 7)
    place = jnp.concatenate([jnp.zeros((1, BP - NC), F32), place.astype(F32)], axis=1)
    send_i[...] = place

    for load in loads[2:6]:
        load.wait()
    regions = regions_ref[...]
    factor = jnp.zeros(regions.shape, F32)
    for k in range(NREG):
        factor = jnp.where(regions == k, inv_ref[0:1, k : k + 1], factor)
    scaled = charges_ref[...] * factor
    rows_ref[pl.ds(0, 16, stride=2), :] = scaled
    rows_ref[pl.ds(1, 16, stride=2), :] = pltpu.roll(scaled, CP, 1)
    charge_rows = rows_ref[...]
    bricks = charge_rows[:, 0:1] * projection_ref[:, 0:BP]
    for p in range(1, CP):
        bricks = bricks + charge_rows[:, p : p + 1] * projection_ref[:, p * BP : (p + 1) * BP]
    send_b[...] = bricks

    pl.semaphore_wait(barrier, ring + line + N_GY - 1)

    def to_ring(j):
        other = away(gx, j, line, 1)
        slot = j * N_X + line
        remote(send_i, recv_i.at[slot], "gx", other, send_sem.at[0], ring_sem.at[0, j])
        remote(send_b, recv_b.at[slot], "gx", other, send_sem.at[1], ring_sem.at[1, j])

    def to_line(index, block, j):
        for i in range(line):
            other = away(gx, ring, i, 1)
            slot = j * N_X + i
            remote(index, recv_i.at[slot], "gx", other, send_sem.at[2], line_sem.at[0, j // 2])
            remote(block, recv_b.at[slot], "gx", other, send_sem.at[3], line_sem.at[1, j // 2])

    for j in (5, 6, 3, 4, 1, 2, 0):
        to_ring(j)
    to_line(send_i, send_b, ring)
    recv_i[last] = place
    recv_b[last] = bricks

    for load in loads[6:9]:
        load.wait()
    shape = (NC, NC)
    eye = rows(shape) == lanes(shape)
    source_col = jnp.sum(
        jnp.where(eye, source_ref[...].astype(F32), 0.0), axis=1, keepdims=True
    )
    from_source = jnp.where(source_col == lanes(shape).astype(F32), 1.0, 0.0)
    near_charges = lax.dot_general(
        from_source, charge_rows, NN, precision=HIGHEST, preferred_element_type=F32
    )
    lower = lanes((NC, BP)) < CP
    near_charges = jnp.where(lower, near_charges, pltpu.roll(near_charges, CP, 1))

    def near_part(p):
        part = tiles_ref[:, p // 2 * BP : (p // 2 + 1) * BP] * near_charges
        return jnp.where(lower if p % 2 == 0 else jnp.logical_not(lower), part, 0.0)

    contrib = lane_sums(near_part, 0, CP)
    contrib = contrib + pltpu.roll(contrib, CP, 1)
    to_target = jnp.where(rows(shape) == target_ref[...], 1.0, 0.0)
    near_ref[...] = lax.dot_general(
        to_target, contrib, NN, precision=HIGHEST, preferred_element_type=F32
    )

    for load in loads[9:14]:
        load.wait()
    point, lane = rows((NC, BP)), lanes((NC, BP))
    for dx in range(4):
        for d in range(4):
            keep = (point // 8 == d) & (point % 8 == lane % 8)
            for part in range(2):
                wave = planes_ref[part * 4 + dx : part * 4 + dx + 1, :]
                c = (d * 2 + part) * BP
                spread_ref[dx * NC : (dx + 1) * NC, c : c + BP] = jnp.where(keep, wave, 0.0)
    high, low = halves(spread_ref[...])
    spread_high_ref[0:BP, :] = high
    spread_high_ref[BP : 2 * BP, :] = high
    spread_low_ref[...] = low
    for c in range(8):
        part = slice(c * BP, (c + 1) * BP)
        gather_ref[part, :] = jnp.concatenate(halves(spread_ref[:, part].T), axis=1)

    for c in range(4):
        part = slice(c * 128, (c + 1) * 128)
        kernel_ref[:, part] = (1.0 / (FULL * FULL * G3)) / (
            along_x_ref[...] + along_y_ref[:, part] + along_z_ref[...]
        )

    for j in (5, 6, 3, 4, 1, 2, 0):
        slot = j * N_X + line
        wait_for(recv_i.at[slot], ring_sem.at[0, j])
        wait_for(recv_b.at[slot], ring_sem.at[1, j])
        to_line(recv_i.at[slot], recv_b.at[slot], j)

    tile = rows((128, 128))
    for g in range(GROUPS - 1, -1, -1):
        wait_for(recv_i.at[0 : 2 * line], line_sem.at[0, g])
        for j in (2 * g, 2 * g + 1):
            where = recv_i[N_X * j + line]
            for i in range(line):
                where = where + pltpu.roll(recv_i[N_X * j + i], NC * (i + 1), 1)
            where = where.astype(jnp.int32)
            at_cell = jnp.where((where & 127) == tile, 1.0, 0.0)
            at_cell_t = at_cell.T.astype(BF16)
            at_plane = jnp.where((where >> 7) == tile, 1.0, 0.0).T.astype(BF16)
            part = slice(j * 128, (j + 1) * 128)
            cells_ref[:, part] = at_cell.astype(BF16)
            cells_t_ref[part, :] = jnp.concatenate([at_cell_t, at_cell_t], axis=1)
            turn_ref[part, :] = dot(at_plane, phases_ref[0], NN) + dot(at_plane, phases_ref[1], NN)
        part = slice(g * SLOTS, (g + 1) * SLOTS)
        wait_for(recv_b.at[0 : 2 * line], line_sem.at[1, g])
        values = halves(recv_b[g * PER_GROUP : (g + 1) * PER_GROUP].reshape(SLOTS, BP))
        both = jnp.concatenate(values, axis=1)
        cosine, sine = turn_ref[part, 0:BP], turn_ref[part, BP : 2 * BP]
        cells = cells_ref[:, part]
        parts = dot(both, spread_high_ref[...], NN) + dot(values[0], spread_low_ref[...], NN)
        placed = []
        for d in range(4):
            c = d * 2 * BP
            placed.append(cosine * parts[:, c : c + BP] + sine * parts[:, c + BP : c + 2 * BP])
        placed = halves(jnp.concatenate(placed, axis=1))
        term = dot(cells, placed[0], NN) + dot(cells, placed[1], NN)
        grid_ref[...] = term if g == GROUPS - 1 else grid_ref[...] + term
    for d in range(4):
        lines = swap_blocks(
            [grid_ref[b * 8 : (b + 1) * 8, d * BP : (d + 1) * BP] for b in range(16)]
        )
        for k in range(16):
            send_g[k, d * 8 : (d + 1) * 8, :] = lines[k]
    send_columns(gy, send_g, recv_g, send_sem.at[4], recv_sem.at[0])
    recv_g[gy] = send_g[gy]

    for load in loads[14:18]:
        load.wait()
    wait_for(recv_g.at[0 : N_GY - 1], recv_sem.at[0])
    turned = recv_g[...].reshape(FULL, ZC).T
    high, low = halves(turned)
    field = dot(jnp.concatenate([high, low], axis=0), hy_ref[0], NN)
    field = field[0:ZC] + field[ZC : 2 * ZC] + dot(high, hy_ref[1], NN)
    high, low = halves(field)
    field = dot(hz_ref[...], jnp.concatenate([high, low], axis=0), NN) + dot(hz_low_ref[...], high, NN)
    high, low = halves(field * kernel_ref[...])
    field = dot(hzt_ref[...], high, NN)
    field = field[0:ZC] + field[ZC : 2 * ZC] + dot(hzt_ref[0:ZC, :], low, NN)
    high, low = halves(field)
    both = jnp.concatenate([high, low], axis=0)
    half = N_GY // 2
    for first in (0, half):
        others = [lax.rem(gy + ORDER[i], N_GY) for i in range(first, first + half)]
        lines = [pl.ds(pl.multiple_of(other * 32, 32), 32) for other in others]
        field = dot(jnp.concatenate([hy_ref[0, part, :] for part in lines], axis=0), both, NT)
        field = (
            field[:, 0:ZC]
            + field[:, ZC : 2 * ZC]
            + dot(jnp.concatenate([hy_ref[1, part, :] for part in lines], axis=0), high, NT)
        )
        for i, other in enumerate(others):
            block = field[i * 32 : (i + 1) * 32, :]
            if first + i < N_GY - 1:
                send_f[first + i] = block
                remote(send_f.at[first + i], recv_f.at[gy], "gy", other, send_sem.at[5], recv_sem.at[1])
            else:
                recv_f[gy] = block
    wait_for(recv_f.at[0 : N_GY - 1], recv_sem.at[1])

    for d in range(4):
        parts = swap_blocks([recv_f[k, d * 8 : (d + 1) * 8, :] for k in range(16)])
        for b in range(16):
            grid_ref[b * 8 : (b + 1) * 8, d * BP : (d + 1) * BP] = parts[b]
    field = jnp.concatenate(halves(grid_ref[...]), axis=0)

    def back_on_line(j):
        for i in range(line):
            other = away(gx, ring, i, -1)
            remote(
                send_q.at[j * N_X + i], recv_q.at[j, i], "gx", other, send_sem.at[6], back_sem.at[j]
            )

    for first, end in ((1, 3), (0, 1), (5, 7), (3, 5), (7, 8)):
        part = slice(first * BP, end * BP)
        lines = dot(cells_t_ref[part, :], field, NN)
        cosine, sine = turn_ref[part, 0:BP], turn_ref[part, BP : 2 * BP]
        turned = []
        for d in range(4):
            turned += [cosine * lines[:, d * BP : (d + 1) * BP], sine * lines[:, d * BP : (d + 1) * BP]]
        lines = halves(jnp.concatenate(turned, axis=1))
        total = dot(lines[0], gather_ref[...], NN)
        total = total[:, 0:BP] + total[:, BP : 2 * BP] + dot(lines[1], gather_ref[:, 0:BP], NN)
        send_q[first * N_X : end * N_X] = total.reshape((end - first) * N_X, NC, BP)
        for j in range(first, end):
            slot = j * N_X
            if j in NEAR:
                other = away(gx, j, line, -1)
                remote(
                    send_q.at[slot + line], recv_r.at[j], "gx", other, send_sem.at[7], recv_sem.at[2]
                )
                near = j - NEAR[0]
                for i in range(line):
                    remote(
                        send_q.at[slot + i],
                        recv_n.at[near, i],
                        "gx",
                        other,
                        send_sem.at[6],
                        near_sem.at[near],
                    )
            elif j < ring:
                back_on_line(j)

    def add_line(j):
        wait_for(recv_q.at[j], back_sem.at[j])
        return send_q[j * N_X + line] + recv_q[j, 0] + recv_q[j, 1] + recv_q[j, 2]

    def back_on_ring(j):
        send_r[j] = add_line(j)
        other = away(gx, j, line, -1)
        remote(send_r.at[j], recv_r.at[j], "gx", other, send_sem.at[7], recv_sem.at[2])

    for j in (1, 2, 0):
        back_on_ring(j)
    for near in range(2):
        wait_for(recv_n.at[near], near_sem.at[near])
    for i in range(line):
        slot = ring * N_X + i
        send_q[slot] = send_q[slot] + recv_n[0, i] + recv_n[1, i]
    back_on_line(ring)

    for j in (3, 4):
        back_on_ring(j)
    samples = add_line(ring)
    wait_for(recv_r, recv_sem.at[2])
    for j in range(ring):
        samples = samples + recv_r[j]

    def far_part(p):
        return projection_ref[:, p * BP : (p + 1) * BP] * samples

    far_field = lane_sums(far_part, 0, CP)
    far_field = far_field + pltpu.roll(far_field, CP, 1)
    rows_ref[...] = far_field + near_ref[...]
    even = rows_ref[pl.ds(0, 16, stride=2), :]
    odd = rows_ref[pl.ds(1, 16, stride=2), :]
    out_ref[...] = jnp.where(lanes((16, BP)) < CP, even, pltpu.roll(odd, CP, 1))

    wait_for(recv_i.at[0:ring], send_sem.at[0])
    wait_for(recv_b.at[0:ring], send_sem.at[1])
    wait_for(recv_i.at[0 : N_Z * line], send_sem.at[2])
    wait_for(recv_b.at[0 : N_Z * line], send_sem.at[3])
    wait_for(send_g.at[0 : N_GY - 1], send_sem.at[4])
    wait_for(send_f.at[0 : N_GY - 1], send_sem.at[5])
    wait_for(send_q.at[0 : N_Z * line], send_sem.at[6])
    wait_for(send_r.at[0:ring], send_sem.at[7])


def on_device(
    charges,
    regions,
    inv_permittivity,
    projection,
    slab_owner,
    brick_index,
    near_tiles,
    near_target,
    near_source,
):
    tables = [jnp.asarray(t) for t in host_tables()]
    in_hbm = pl.BlockSpec(memory_space=pltpu.HBM)
    small = pltpu.VMEM((1, NC), jnp.int32)
    bricks = pltpu.VMEM((N_GX, NC, BP), F32)
    columns = pltpu.VMEM((N_GY, 32, ZC), F32)
    out = pl.pallas_call(
        body,
        out_shape=jax.ShapeDtypeStruct((16, BP), F32),
        in_specs=[in_hbm] * 18,
        out_specs=pl.BlockSpec(memory_space=pltpu.VMEM),
        scratch_shapes=[
            pltpu.VMEM((16, BP), F32),
            pltpu.VMEM((16, BP), jnp.int32),
            pltpu.VMEM((1, NREG), F32),
            small,
            small,
            small,
            small,
            pltpu.VMEM((NC, CP * BP), F32),
            pltpu.VMEM((NC, CP * CP), F32),
            pltpu.VMEM((2, FULL, FULL), BF16),
            pltpu.VMEM((G3, 2 * ZC), BF16),
            pltpu.VMEM((G3, ZC), BF16),
            pltpu.VMEM((2 * ZC, G3), BF16),
            pltpu.VMEM((2, 128, 2 * BP), BF16),
            pltpu.VMEM((8, BP), F32),
            pltpu.VMEM((1, BP), F32),
            pltpu.VMEM((1, FULL), F32),
            pltpu.VMEM((G3, BP), F32),
            pltpu.VMEM((NC, BP), F32),
            pltpu.VMEM((NC, BP), F32),
            pltpu.VMEM((G3, FULL), F32),
            pltpu.VMEM((N_GX * NC, 2 * BP), F32),
            pltpu.VMEM((128, N_GX * NC), BF16),
            pltpu.VMEM((N_GX * NC, 2 * 128), BF16),
            pltpu.VMEM((BP, 2 * FULL), F32),
            pltpu.VMEM((2 * BP, 2 * FULL), BF16),
            pltpu.VMEM((BP, 2 * FULL), BF16),
            pltpu.VMEM((2 * FULL, 2 * BP), BF16),
            pltpu.VMEM((128, FULL), F32),
            pltpu.VMEM((1, BP), F32),
            pltpu.VMEM((N_GX, 1, BP), F32),
            pltpu.VMEM((NC, BP), F32),
            bricks,
            columns,
            columns,
            columns,
            columns,
            bricks,
            pltpu.VMEM((N_Z, N_X - 1, NC, BP), F32),
            pltpu.VMEM((N_Z - 1, NC, BP), F32),
            pltpu.VMEM((N_Z - 1, NC, BP), F32),
            pltpu.VMEM((2, N_X - 1, NC, BP), F32),
            pltpu.SemaphoreType.DMA((18,)),
            pltpu.SemaphoreType.DMA((8,)),
            pltpu.SemaphoreType.DMA((3,)),
            pltpu.SemaphoreType.DMA((2, N_Z - 1)),
            pltpu.SemaphoreType.DMA((2, N_Z - 1)),
            pltpu.SemaphoreType.DMA((2, N_X - 1)),
            pltpu.SemaphoreType.DMA((N_Z,)),
            pltpu.SemaphoreType.DMA((2,)),
        ],
        compiler_params=pltpu.CompilerParams(
            collective_id=0, has_side_effects=True, vmem_limit_bytes=60 * 1024 * 1024
        ),
    )(
        charges.reshape(16, BP),
        regions.reshape(16, BP),
        inv_permittivity.reshape(1, NREG),
        slab_owner.reshape(1, NC),
        brick_index.reshape(1, NC),
        near_target.reshape(1, NC),
        near_source.reshape(1, NC),
        projection,
        near_tiles,
        *tables,
    )
    return out.reshape(-1)


def solution(mesh):
    both = P(("gx", "gy"))
    wide = P(("gx", "gy"), None)
    return jax.shard_map(
        on_device,
        mesh=mesh,
        in_specs=(both, both, P(), wide, both, both, wide, both, both),
        out_specs=both,
        check_vma=False,
    )
```
